256 devices in a mesh: replica: 16 (over y_lo, z), section: 4 (over y_hi, core), shard: 4 (over x).
Axes of the slice: x: 4, y: 4 (y_hi: 2, y_lo: 2; y = y_hi * 2 + y_lo), z: 8, core: 2. Of those that a mesh axis runs over, the one named last changes fastest.
Arguments:
- inputs: bfloat16 [16, 1, 128, 1024], P('replica', None, None, 'shard'), may hold values from -17 to 17
- targets: bfloat16 [16, 1, 128, 1024], P('replica', None, None, 'shard'), may hold values from -6 to 6
- weight_a: bfloat16 [16, 4, 1024, 3072], P('replica', 'section', None, 'shard'), may hold values from -6 to 6
- weight_b: bfloat16 [16, 4, 3072, 1024], P('replica', 'section', 'shard'), may hold values from -6 to 6
- moment_a: bfloat16 [16, 4, 1024, 3072], P('replica', 'section', None, 'shard'), may hold values from -3 to 3
- moment_b: bfloat16 [16, 4, 3072, 1024], P('replica', 'section', 'shard'), may hold values from -3 to 3
- routes: int32 [1, 3, 16, 16], replicated, may hold values from 0 to 15, each once within a row
- partners: int32 [4, 2, 16, 16], replicated, may hold values from 0 to 15, as said below
Outputs:
- new_weight_a: bfloat16 [16, 4, 1024, 3072], P('replica', 'section', None, 'shard')
- new_weight_b: bfloat16 [16, 4, 3072, 1024], P('replica', 'section', 'shard')
- new_moment_a: bfloat16 [16, 4, 1024, 3072], P('replica', 'section', None, 'shard')
- new_moment_b: bfloat16 [16, 4, 3072, 1024], P('replica', 'section', 'shard')
The draws below stay inside these ranges and needn't reach their ends.
Inputs may be any that keep to these rules, and one draw needn't show every extreme that they name: Each routes[m, s, q, :] names every replica once, so each replica of section s + 1 receives exactly one block from every replica of section s. For each section s, projection t and piece k, partners[s, t, k, :] is its own inverse (the partner of the partner is the replica itself); for each s, t and replica r, partners[s, t, :, r] names every replica once, and exactly one piece pairs r with itself.
All inputs are finite; a program needn't handle non-finite values.
Results may differ from the reference program's by a relative error of at most 0.022.
Values may be sent and summed in bfloat16 or wider, within the bound.
A program may use at most 128 MiB of HBM per device.

```python
import jax
import jax.numpy as jnp
from jax import lax

D = 1024
K = 3072
B = 128
M = 1
REPLICAS = 16
SECTIONS = 4
N_REPLICA = 16
N_SECTION = 4
N_SHARD = 4


def draw_inputs(key, part):
    key = jax.random.fold_in(key, 3)
    first, second, third = jax.random.split(key, 3)
    row_scale = jnp.exp(jax.random.uniform(second, (REPLICAS, M, B, 1), jnp.float32, -1.0, 1.0))
    position = jnp.arange(D, dtype=jnp.float32) / (D - 1.0) * 2.0 - 1.0
    ramp = jnp.exp(0.8 * position)
    column_scale = jnp.exp(jax.random.uniform(third, (D,), jnp.float32, -0.6, 0.6)) * ramp
    base = jnp.clip(jax.random.normal(first, (REPLICAS, M, B, D), jnp.float32), -5.0, 5.0)
    return (base * row_scale * column_scale * 0.3).astype(jnp.bfloat16)


def pairing_table(key):
    first, second = jax.random.split(key)
    labels = jax.random.permutation(first, REPLICAS).astype(jnp.int32)
    inverse = jnp.argsort(labels, stable=True).astype(jnp.int32)
    offsets = jax.random.permutation(second, REPLICAS).astype(jnp.int32)
    mixed = jnp.bitwise_xor(labels[None, :], offsets[:, None])
    return inverse[mixed].astype(jnp.int32)


def draw_partners(key, part):
    key = jax.random.fold_in(key, 7)
    keys = jax.random.split(key, SECTIONS * 2)
    tables = jax.vmap(pairing_table)(keys)
    return tables.reshape(SECTIONS, 2, REPLICAS, REPLICAS).astype(jnp.int32)


def block_scale(stream_key, extent, cuts, least, high):
    factor_of = 1.0
    for dim, blocks in cuts:
        draws = jax.random.uniform(jax.random.fold_in(jax.random.fold_in(stream_key, 6), dim), (blocks,), jnp.float32, least / len(cuts), high / len(cuts))
        factor_of = factor_of * jnp.repeat(jnp.exp(draws), extent[dim] // blocks).reshape((-1,) + (1,) * (len(extent) - 1 - dim))
    return factor_of


def gaussian(stream_key, shape, spread, limit, pieces=(), kind=jnp.bfloat16):
    loudness = block_scale(stream_key, shape, pieces, -0.22, 0.18) if pieces else 1.0
    drawn = jax.random.normal(stream_key, shape, jnp.float32) * spread * loudness
    return jnp.minimum(jnp.maximum(drawn, -limit), limit).astype(kind)


def setup_inputs(seed: int = 0) -> dict:
    key_list = jax.random.split(jax.random.key(seed), 9)
    return {
        "inputs": draw_inputs(jax.random.fold_in(key_list[8], 71), 0),
        "targets": gaussian(key_list[1], (REPLICAS, M, B, D), 1.0, 6.0, ((0, 16), (3, 4))),
        "weight_a": gaussian(key_list[2], (REPLICAS, SECTIONS, D, K), 1.0, 6.0, ((0, 16), (1, 4), (3, 4))),
        "weight_b": gaussian(key_list[3], (REPLICAS, SECTIONS, K, D), 1.0, 6.0, ((0, 16), (1, 4), (2, 4))),
        "moment_a": gaussian(key_list[4], (REPLICAS, SECTIONS, D, K), 0.5, 3.0, ((0, 16), (1, 4), (3, 4))),
        "moment_b": gaussian(key_list[5], (REPLICAS, SECTIONS, K, D), 0.5, 3.0, ((0, 16), (1, 4), (2, 4))),
        "routes": jax.vmap(lambda own: jax.random.permutation(own, REPLICAS))(jax.random.split(key_list[6], M * (SECTIONS - 1) * REPLICAS)).reshape((M, SECTIONS - 1, REPLICAS, REPLICAS)).astype(jnp.int32),
        "partners": draw_partners(jax.random.fold_in(key_list[8], 71), 0),
    }


epsilon = 1e-05
inner_rate = 0.5
momentum_decay = 0.9
outer_rate = 0.7

def rounded(value):
    return lax.optimization_barrier(value.astype(jnp.bfloat16)).astype(jnp.float32)

def block_forward(section_input, weight_in, weight_out):
    scale_in = 1.0 / D ** 0.5
    scale_out = 1.0 / K ** 0.5
    wide = section_input.astype(jnp.float32)
    inverse_rms = lax.rsqrt(lax.optimization_barrier(jnp.mean(wide * wide, axis=-1, keepdims=True)) + epsilon)
    normed = (wide * inverse_rms).astype(jnp.bfloat16)
    preact = jnp.einsum('rmbd,rdk->rmbk', normed.astype(jnp.float32), weight_in.astype(jnp.float32)) * scale_in
    hidden = jax.nn.silu(preact).astype(jnp.bfloat16)
    share = K // N_SHARD
    total = jnp.zeros(wide.shape, jnp.float32)
    for index in range(N_SHARD):
        part_hidden = hidden[..., index * share:(index + 1) * share].astype(jnp.float32)
        part_weight = weight_out[:, index * share:(index + 1) * share, :].astype(jnp.float32)
        total = total + rounded(jnp.einsum('rmbk,rkd->rmbd', part_hidden, part_weight) * scale_out)
    output = (wide + total).astype(jnp.bfloat16)
    return (output, normed, preact, hidden, inverse_rms)

def block_backward(section_input, normed, preact, hidden, inverse_rms, weight_in, weight_out, upstream):
    scale_in = 1.0 / D ** 0.5
    scale_out = 1.0 / K ** 0.5
    up_wide = upstream.astype(jnp.float32)
    grad_out = jnp.einsum('rmbk,rmbd->rkd', hidden.astype(jnp.float32), up_wide) * scale_out
    grad_hidden = jnp.einsum('rmbd,rkd->rmbk', up_wide, weight_out.astype(jnp.float32)) * scale_out
    gate = jax.nn.sigmoid(preact)
    grad_pre = (grad_hidden * gate * (1.0 + preact * (1.0 - gate))).astype(jnp.bfloat16)
    grad_in = jnp.einsum('rmbd,rmbk->rdk', normed.astype(jnp.float32), grad_pre.astype(jnp.float32)) * scale_in
    share = K // N_SHARD
    total = jnp.zeros(up_wide.shape, jnp.float32)
    for index in range(N_SHARD):
        part_grad = grad_pre[..., index * share:(index + 1) * share].astype(jnp.float32)
        part_weight = weight_in[:, :, index * share:(index + 1) * share].astype(jnp.float32)
        total = total + rounded(jnp.einsum('rmbk,rdk->rmbd', part_grad, part_weight) * scale_in)
    exact = section_input.astype(jnp.float32) * inverse_rms
    along = lax.optimization_barrier(jnp.mean(total * exact, axis=-1, keepdims=True))
    result = (up_wide + inverse_rms * (total - exact * along)).astype(jnp.bfloat16)
    return (result, grad_in, grad_out)

def target_slots(table):
    labels = jnp.arange(N_REPLICA, dtype=jnp.int32)
    match = (table[..., None, :] == labels[:, None]).astype(jnp.int32)
    return lax.optimization_barrier(jnp.sum(match * labels, axis=-1))

def route_forward(values, table):
    group_rows = B // N_REPLICA
    grouped = values.reshape(N_REPLICA, M, N_REPLICA, group_rows, D)
    slots = jnp.transpose(target_slots(table), (1, 0, 2))
    picked = jnp.take_along_axis(grouped, slots[:, :, :, None, None], axis=2)
    return jnp.transpose(picked, (2, 1, 0, 3, 4)).reshape(N_REPLICA, M, B, D)

def route_back(values, table):
    group_rows = B // N_REPLICA
    grouped = jnp.transpose(values.reshape(N_REPLICA, M, N_REPLICA, group_rows, D), (2, 1, 0, 3, 4))
    slots = jnp.transpose(table, (1, 0, 2))
    picked = jnp.take_along_axis(grouped, slots[:, :, :, None, None], axis=2)
    return picked.reshape(N_REPLICA, M, B, D)

def partner_view(array, axis, partners):
    taken = [jnp.take(jnp.take(array, index, axis=axis), partners[index], axis=0) for index in range(N_REPLICA)]
    return jnp.stack(taken, axis=axis)

def outer_update(weights, moments, grads, partners, shape, axis):
    initial = weights.shape
    deltas = (inner_rate * grads).astype(jnp.bfloat16).reshape(shape)
    weights = weights.reshape(shape)
    moments = moments.reshape(shape)
    mean_weight = (weights.astype(jnp.float32) + partner_view(weights, axis, partners).astype(jnp.float32)) * 0.5
    mean_moment = (moments.astype(jnp.float32) + partner_view(moments, axis, partners).astype(jnp.float32)) * 0.5
    mean_delta = (deltas.astype(jnp.float32) + partner_view(deltas, axis, partners).astype(jnp.float32)) * 0.5
    new_moment = momentum_decay * mean_moment + mean_delta
    new_weight = mean_weight - outer_rate * (momentum_decay * new_moment + mean_delta)
    return (new_weight.astype(jnp.bfloat16).reshape(initial), new_moment.astype(jnp.bfloat16).reshape(initial))

def reference(inputs, targets, weight_a, weight_b, moment_a, moment_b, routes, partners):
    current = inputs
    saved = []
    final = inputs
    for section in range(N_SECTION):
        results = block_forward(current, weight_a[:, section], weight_b[:, section])
        saved.append((current,) + results[1:])
        final = results[0]
        if section + 1 < N_SECTION:
            current = route_forward(final, routes[:, section])
    upstream = (final.astype(jnp.float32) - targets.astype(jnp.float32)).astype(jnp.bfloat16)
    weights_in, weights_out, moments_in, moments_out = ([], [], [], [])
    shape_in = (N_REPLICA, N_REPLICA, D // N_REPLICA, K)
    shape_out = (N_REPLICA, N_SHARD, N_REPLICA, K // (N_SHARD * N_REPLICA), D)
    for section in reversed(range(N_SECTION)):
        section_input, normed, preact, hidden, inverse_rms = saved[section]
        result, grad_in, grad_out = block_backward(section_input, normed, preact, hidden, inverse_rms, weight_a[:, section], weight_b[:, section], upstream)
        new_in, moment_in = outer_update(weight_a[:, section], moment_a[:, section], grad_in, partners[section, 0], shape_in, 1)
        new_out, moment_out = outer_update(weight_b[:, section], moment_b[:, section], grad_out, partners[section, 1], shape_out, 2)
        weights_in.insert(0, new_in)
        weights_out.insert(0, new_out)
        moments_in.insert(0, moment_in)
        moments_out.insert(0, moment_out)
        if section > 0:
            upstream = route_back(result, routes[:, section - 1])
    return (jnp.stack(weights_in, axis=1), jnp.stack(weights_out, axis=1), jnp.stack(moments_in, axis=1), jnp.stack(moments_out, axis=1))
```

```python
import functools
import math

import jax
import jax.numpy as jnp
from jax import lax
from jax.experimental import pallas as pl
from jax.experimental.pallas import tpu as pltpu
from jax.sharding import PartitionSpec as P

MESH = pl.DeviceIdType.MESH
f32 = jnp.float32
bf16 = jnp.bfloat16

epsilon = 1e-05
inner_rate = 0.5
momentum_decay = 0.9
outer_rate = 0.7

step_size = outer_rate * (1.0 + momentum_decay)
mix_rate = step_size * momentum_decay - outer_rate * momentum_decay * momentum_decay

REPLICAS = 16
SECTIONS = 4
SHARDS = 4
ROWS = 128
GROUP = ROWS // REPLICAS
WIDTH = 1024
FEATURES = WIDTH // SHARDS
HIDDEN = 768
PIECE_A = WIDTH // REPLICAS
PIECE_B = HIDDEN // REPLICAS
scale_in = 1.0 / math.sqrt(WIDTH)
scale_out = 1.0 / math.sqrt(HIDDEN * SHARDS)

NN = (((1,), (0,)), ((), ()))
NT = (((1,), (1,)), ((), ()))


def dot(a, b, dims=NN):
    return lax.dot_general(a, b, dims, preferred_element_type=f32)


def pack_rows(wide):
    return jnp.concatenate([wide[:, :, :128], wide[:, :, 128:]], axis=1).astype(bf16)


def unpack_rows(packed):
    wide = packed.astype(f32)
    count = wide.shape[0]
    return jnp.concatenate(
        [
            wide[:, :GROUP, :].reshape(count * GROUP, 128),
            wide[:, GROUP:, :].reshape(count * GROUP, 128),
        ],
        axis=1,
    )


def kernel(
    inp_h, tgt_h, wa_h, wb_h, ma_h, mb_h, routes, partners,
    nwa_h, nwb_h, nma_h, nmb_h,
    inp, tgt, wa, wb, ma, mb,
    fwd_all, fwd_term, fwd_got, fwd_out, fwd_send, fwd_recv,
    bwd_all, bwd_term, bwd_got, bwd_send, bwd_recv, along_send, along_got, up_own,
    inv_rms, slope, hidden_t, normed_t, grad_pre, grad_a, grad_b,
    qa_send, qb_send, qa_recv, qb_recv, va_send, vb_send, va_recv, vb_recv,
    order_f, order_a, order_b,
    load_sem, store_sem, x_send, x_recv, z_send, z_recv, bulk_send, bulk_recv,
):
    r = lax.axis_index("replica")
    s = lax.axis_index("section")
    x = lax.axis_index("shard")
    y, z = r // 8, lax.rem(r, 8)
    first, last = s == 0, s == SECTIONS - 1

    def other_shard(d):
        return lax.rem(x + d, SHARDS)

    def peer(t):
        dy, h = lax.rem(t, 2), t // 2
        odd = lax.rem(h, 2)
        dz = odd * ((h + 1) // 2) + (1 - odd) * lax.rem(8 - h // 2, 8)
        return lax.rem(y + dy, 2) * 8 + lax.rem(z + dz, 8)

    def each(count, body, start=0):
        def step(i, carry):
            body(i)
            return carry

        lax.fori_loop(start, count, step, 0)

    loads = [
        pltpu.make_async_copy(src, dst, load_sem.at[i])
        for i, (src, dst) in enumerate(
            [(inp_h, inp), (wa_h, wa), (wb_h, wb), (ma_h, ma), (mb_h, mb), (tgt_h, tgt)]
        )
    ]
    for copy in loads:
        copy.start()

    barrier = pltpu.get_barrier_semaphore()

    def greet(device):
        pl.semaphore_signal(barrier, inc=1, device_id=device, device_id_type=MESH)

    for d in (1, 2, 3):
        greet((r, s, other_shard(d)))

    @pl.when(s < SECTIONS - 1)
    def _():
        each(REPLICAS, lambda t: greet((peer(t), s + 1, x)))

    @pl.when(s > 0)
    def _():
        each(REPLICAS, lambda t: greet((peer(t), s - 1, x)))

    each(REPLICAS, lambda t: greet((peer(t), s, x)), 1)

    links = jnp.minimum(s, 1) + jnp.minimum(SECTIONS - 1 - s, 1)
    pl.semaphore_wait(barrier, SHARDS - 1 + REPLICAS - 1 + REPLICAS * links)


    def gather_copy(ref, phase, d):
        return pltpu.make_async_remote_copy(
            ref.at[x], ref.at[x], x_send.at[phase, d], x_recv.at[phase, d],
            device_id=(r, s, other_shard(d)), device_id_type=MESH,
        )

    def scatter_copy(src, dst, phase, d):
        return pltpu.make_async_remote_copy(
            src.at[other_shard(d)], dst.at[x], x_send.at[phase, d], x_recv.at[phase, d],
            device_id=(r, s, other_shard(d)), device_id_type=MESH,
        )

    def route_copy(src, slot, dst, phase, t, section):
        return pltpu.make_async_remote_copy(
            src.at[slot], dst.at[r], z_send.at[phase], z_recv.at[phase],
            device_id=(peer(t), section, x), device_id_type=MESH,
        )

    def route_wait_recv(dst, phase):
        pltpu.make_async_copy(dst, dst, z_recv.at[phase]).wait()

    def route_wait_send(src, phase):
        pltpu.make_async_copy(src, src, z_send.at[phase]).wait()

    def bulk_start(src, dst, which):
        def body(t):
            p = peer(t)
            pltpu.make_async_remote_copy(
                src.at[p], dst.at[r], bulk_send.at[which], bulk_recv.at[which],
                device_id=(p, s, x), device_id_type=MESH,
            ).start()

        each(REPLICAS, body, 1)

    def bulk_wait_recv(dst, which):
        part = dst.at[0 : REPLICAS - 1]
        pltpu.make_async_copy(part, part, bulk_recv.at[which]).wait()

    def bulk_wait_send(src, which):
        part = src.at[0 : REPLICAS - 1]
        pltpu.make_async_copy(part, part, bulk_send.at[which]).wait()


    def invert(table, out):
        def body(p):
            found = 0
            for g in range(REPLICAS):
                apart = table(g) - p
                found = jnp.maximum(found, g * (1 - jnp.minimum(apart * apart, 1)))
            out[p] = found

        each(REPLICAS, body)

    link = jnp.minimum(s, SECTIONS - 2)


    def fill_q(w, m, order, send, recv):
        def body(p):
            k = order[p]
            value = (w[k].astype(f32) + mix_rate * m[k].astype(f32)).astype(bf16)
            send[p] = value

        each(REPLICAS, body)
        recv[r] = send[r]

    def fill_v(m, grad, factor, order, send, recv):
        def body(p):
            k = order[p]
            value = momentum_decay * m[k].astype(f32) + factor * grad[k]
            send[p] = value.astype(bf16)

        each(REPLICAS, body)
        recv[r] = send[r]

    def prepare_q():
        invert(lambda g: partners[s, 0, g, r], order_a)
        invert(lambda g: partners[s, 1, g, r], order_b)
        loads[3].wait()
        loads[4].wait()
        fill_q(wb, mb, order_b, qb_send, qb_recv)
        fill_q(wa, ma, order_a, qa_send, qa_recv)

    def rows_a(j):
        span = FEATURES // PIECE_A
        return wa[pl.ds(j * span, span)].reshape(FEATURES, HIDDEN)

    def columns_b(j):
        columns = pl.ds(pl.multiple_of(j * FEATURES, FEATURES), FEATURES)
        return wb[:, :, columns].reshape(HIDDEN, FEATURES)


    loads[0].wait()

    @pl.when(first)
    def _():
        fwd_all[x] = inp[...]

    @pl.when(s > 0)
    def _():
        loads[1].wait()
        loads[2].wait()
        prepare_q()

    @pl.when(s >= 2)
    def _():
        bulk_start(qb_send, qb_recv, 0)

    @pl.when(last)
    def _():
        bulk_start(qa_send, qa_recv, 1)

    @pl.when(s > 0)
    def _():
        invert(lambda g: routes[link, r, g], order_f)
        route_wait_recv(fwd_recv, 0)
        fwd_all[x] = unpack_rows(fwd_recv[...]).astype(bf16)

    for d in (2, 1, 3):
        gather_copy(fwd_all, 0, d).start()

    @pl.when(first)
    def _():
        invert(lambda g: routes[link, r, g], order_f)
        loads[1].wait()
        loads[2].wait()

    preact = jnp.zeros((ROWS, HIDDEN), f32)
    square = jnp.zeros((ROWS, 1), f32)
    for d in (0, 1, 3, 2):
        if d:
            gather_copy(fwd_all, 0, d).wait_recv()
        j = lax.rem(x + SHARDS - d, SHARDS)
        part = fwd_all[j]
        preact = preact + dot(part, rows_a(j))
        wide = part.astype(f32)
        square = square + jnp.sum(wide * wide, axis=1, keepdims=True)
    inverse = lax.rsqrt(square * (1.0 / WIDTH) + epsilon)
    inv_rms[...] = jnp.broadcast_to(inverse, inv_rms.shape)
    preact = preact * (inverse * scale_in)
    gate = 1.0 / (1.0 + jnp.exp(-preact))
    hidden = (preact * gate).astype(bf16)
    slope[...] = (gate * (1.0 + preact * (1.0 - gate))) * scale_out
    for d in (2, 1, 3, 0):
        j = other_shard(d)
        fwd_term[j] = (dot(hidden, columns_b(j)) * scale_out).astype(bf16)
        if d:
            scatter_copy(fwd_term, fwd_got, 1, d).start()
    total = fwd_term[x].astype(f32)
    for d in (1, 3, 2):
        scatter_copy(fwd_term, fwd_got, 1, d).wait_recv()
        total = total + fwd_got[lax.rem(x + SHARDS - d, SHARDS)].astype(f32)
    output = (fwd_all[x].astype(f32) + total).astype(bf16).astype(f32)

    @pl.when(s < SECTIONS - 1)
    def _():
        fwd_out[...] = output.reshape(REPLICAS, GROUP, FEATURES)
        for t in range(REPLICAS - 1, -1, -1):
            block = fwd_out[order_f[peer(t)]]
            fwd_send[t] = pack_rows(block[None])[0]
            route_copy(fwd_send, t, fwd_recv, 0, t, s + 1).start()

    @pl.when(last)
    def _():
        loads[5].wait()
        up = (output - tgt[...].astype(f32)).astype(bf16)
        bwd_all[x] = up
        up_own[...] = up.astype(f32)
        for d in (2, 1, 3):
            gather_copy(bwd_all, 2, d).start()


    @pl.when(first)
    def _():
        prepare_q()
        bulk_start(qb_send, qb_recv, 0)

    @pl.when(s == 1)
    def _():
        bulk_start(qb_send, qb_recv, 0)

    @pl.when(s < SECTIONS - 1)
    def _():
        loads[5].wait()
        bulk_start(qa_send, qa_recv, 1)

    hidden_t[...] = hidden.T
    for j in range(SHARDS):
        normed = (fwd_all[j].astype(f32) * inverse).astype(bf16)
        normed_t[j * FEATURES : (j + 1) * FEATURES, :] = normed.T


    @pl.when(s < SECTIONS - 1)
    def _():
        route_wait_recv(bwd_recv, 1)
        for g in range(REPLICAS):
            block = bwd_recv[routes[link, r, g]]
            up_own[g * GROUP : (g + 1) * GROUP, :] = unpack_rows(block[None])
        bwd_all[x] = up_own[...].astype(bf16)
        for d in (2, 1, 3):
            gather_copy(bwd_all, 2, d).start()

    grad_hidden = jnp.zeros((ROWS, HIDDEN), f32)
    for d in (0, 1, 3, 2):
        if d:
            gather_copy(bwd_all, 2, d).wait_recv()
        j = lax.rem(x + SHARDS - d, SHARDS)
        grad_hidden = grad_hidden + dot(bwd_all[j], columns_b(j), NT)
    grad_pre[...] = (grad_hidden * slope[...]).astype(bf16)

    def outer_b():
        for j in range(SHARDS):
            value = dot(hidden_t[...], bwd_all[j]).reshape(REPLICAS, PIECE_B, FEATURES)
            grad_b[:, :, j * FEATURES : (j + 1) * FEATURES] = value
        fill_v(mb, grad_b, inner_rate * scale_out, order_b, vb_send, vb_recv)
        bulk_start(vb_send, vb_recv, 2)

    def outer_a():
        for j in range(SHARDS):
            value = dot(normed_t[j * FEATURES : (j + 1) * FEATURES, :], grad_pre[...])
            span = FEATURES // PIECE_A
            grad_a[j * span : (j + 1) * span] = value.reshape(span, PIECE_A, HIDDEN)
        fill_v(ma, grad_a, inner_rate * scale_in, order_a, va_send, va_recv)
        bulk_start(va_send, va_recv, 3)

    @pl.when(s > 0)
    def _():
        inverse = inv_rms[:, :1]
        share = jnp.zeros((ROWS, 1), f32)
        for d in (2, 1, 3, 0):
            j = other_shard(d)
            term = (dot(grad_pre[...], rows_a(j), NT) * scale_in).astype(bf16)
            bwd_term[j] = term
            if d:
                scatter_copy(bwd_term, bwd_got, 3, d).start()
            exact = fwd_all[j].astype(f32) * inverse
            share = share + jnp.sum(term.astype(f32) * exact, axis=1, keepdims=True)
        diagonal = lax.broadcasted_iota(jnp.int32, (ROWS, ROWS), 0) == lax.broadcasted_iota(
            jnp.int32, (ROWS, ROWS), 1
        )
        row = jnp.sum(jnp.where(diagonal, share, 0.0), axis=0, keepdims=True)
        along_send[...] = jnp.broadcast_to(row, along_send.shape)

        def along_copy(d):
            return pltpu.make_async_remote_copy(
                along_send, along_got.at[x], x_send.at[4, d], x_recv.at[4, d],
                device_id=(r, s, other_shard(d)), device_id_type=MESH,
            )

        for d in (2, 1, 3):
            along_copy(d).start()
        total = bwd_term[x].astype(f32)
        for d in (1, 3, 2):
            scatter_copy(bwd_term, bwd_got, 3, d).wait_recv()
            total = total + bwd_got[lax.rem(x + SHARDS - d, SHARDS)].astype(f32)
        for d in (1, 3, 2):
            along_copy(d).wait_recv()
            row = row + along_got[lax.rem(x + SHARDS - d, SHARDS)][:1, :]
        along = jnp.sum(jnp.where(diagonal, row, 0.0), axis=1, keepdims=True) * (1.0 / WIDTH)
        exact = fwd_all[x].astype(f32) * inverse
        result = up_own[...] + inverse * (total - exact * along)
        bwd_send[...] = pack_rows(result.reshape(REPLICAS, GROUP, FEATURES))
        for t in range(REPLICAS - 1, -1, -1):
            route_copy(bwd_send, peer(t), bwd_recv, 1, t, s - 1).start()
        for d in (1, 3, 2):
            scatter_copy(bwd_term, bwd_got, 3, d).wait_send()
            along_copy(d).wait_send()

    outer_b()
    outer_a()


    def outer_step(w, m, grad, factor, table, q_recv, v_recv):
        def body(k):
            partner = partners[s, table, k, r]
            weight = w[k].astype(f32)
            moment = m[k].astype(f32)
            own = momentum_decay * moment + factor * grad[k]
            new_moment = 0.5 * (own + v_recv[partner].astype(f32))
            kept = 0.5 * (weight + mix_rate * moment + q_recv[partner].astype(f32))
            w[k] = (kept - step_size * new_moment).astype(bf16)
            m[k] = new_moment.astype(bf16)

        each(REPLICAS, body)

    bulk_wait_recv(qb_recv, 0)
    bulk_wait_recv(vb_recv, 2)
    outer_step(wb, mb, grad_b, inner_rate * scale_out, 1, qb_recv, vb_recv)
    stores = [
        pltpu.make_async_copy(src, dst, store_sem.at[i])
        for i, (src, dst) in enumerate([(wb, nwb_h), (mb, nmb_h), (wa, nwa_h), (ma, nma_h)])
    ]
    stores[0].start()
    stores[1].start()
    bulk_wait_recv(qa_recv, 1)
    bulk_wait_recv(va_recv, 3)
    outer_step(wa, ma, grad_a, inner_rate * scale_in, 0, qa_recv, va_recv)
    stores[2].start()
    stores[3].start()

    for d in (1, 2, 3):
        gather_copy(fwd_all, 0, d).wait_send()
        scatter_copy(fwd_term, fwd_got, 1, d).wait_send()
        gather_copy(bwd_all, 2, d).wait_send()

    @pl.when(s < SECTIONS - 1)
    def _():
        route_wait_send(fwd_send, 0)

    @pl.when(s > 0)
    def _():
        route_wait_send(bwd_send, 1)

    for which, src in enumerate((qb_send, qa_send, vb_send, va_send)):
        bulk_wait_send(src, which)
    for copy in stores:
        copy.wait()


def per_device(inputs, targets, weight_a, weight_b, moment_a, moment_b, routes, partners):
    def vmem(*shape, dtype=bf16):
        return pltpu.VMEM(shape, dtype)

    shards = (SHARDS, ROWS, FEATURES)
    routed = (REPLICAS, 2 * GROUP, 128)
    bulk_a = (REPLICAS, PIECE_A, HIDDEN)
    bulk_b = (REPLICAS, PIECE_B, WIDTH)
    dma = pltpu.SemaphoreType.DMA
    shape_a = jax.ShapeDtypeStruct(bulk_a, bf16)
    shape_b = jax.ShapeDtypeStruct(bulk_b, bf16)
    anywhere = pl.BlockSpec(memory_space=pl.ANY)
    smem = pl.BlockSpec(memory_space=pltpu.SMEM)
    new_wa, new_wb, new_ma, new_mb = pl.pallas_call(
        kernel,
        out_shape=(shape_a, shape_b, shape_a, shape_b),
        in_specs=[anywhere] * 6 + [smem, smem],
        out_specs=(anywhere,) * 4,
        scratch_shapes=[
            vmem(ROWS, FEATURES), vmem(ROWS, FEATURES),
            vmem(*bulk_a), vmem(*bulk_b), vmem(*bulk_a), vmem(*bulk_b),
            vmem(*shards), vmem(*shards), vmem(*shards), vmem(REPLICAS, GROUP, FEATURES, dtype=f32),
            vmem(*routed), vmem(*routed),
            vmem(*shards), vmem(*shards), vmem(*shards), vmem(*routed), vmem(*routed),
            vmem(8, ROWS, dtype=f32), vmem(SHARDS, 8, ROWS, dtype=f32),
            vmem(ROWS, FEATURES, dtype=f32),
            vmem(ROWS, 128, dtype=f32), vmem(ROWS, HIDDEN, dtype=f32),
            vmem(HIDDEN, ROWS), vmem(WIDTH, ROWS), vmem(ROWS, HIDDEN),
            vmem(*bulk_a, dtype=f32), vmem(*bulk_b, dtype=f32),
            vmem(*bulk_a), vmem(*bulk_b), vmem(*bulk_a), vmem(*bulk_b),
            vmem(*bulk_a), vmem(*bulk_b), vmem(*bulk_a), vmem(*bulk_b),
            pltpu.SMEM((REPLICAS,), jnp.int32), pltpu.SMEM((REPLICAS,), jnp.int32),
            pltpu.SMEM((REPLICAS,), jnp.int32),
            dma((6,)), dma((4,)), dma((5, SHARDS)), dma((5, SHARDS)), dma((2,)), dma((2,)),
            dma((4,)), dma((4,)),
        ],
        compiler_params=pltpu.CompilerParams(
            collective_id=0, has_side_effects=True, vmem_limit_bytes=56 * 2**20
        ),
    )(
        inputs[0, 0], targets[0, 0], weight_a.reshape(bulk_a), weight_b.reshape(bulk_b),
        moment_a.reshape(bulk_a), moment_b.reshape(bulk_b), routes[0], partners,
    )
    return (
        new_wa.reshape(weight_a.shape), new_wb.reshape(weight_b.shape),
        new_ma.reshape(moment_a.shape), new_mb.reshape(moment_b.shape),
    )


def solution(mesh):
    placed = (
        P("replica", None, None, "shard"),
        P("replica", None, None, "shard"),
        P("replica", "section", None, "shard"),
        P("replica", "section", "shard", None),
        P("replica", "section", None, "shard"),
        P("replica", "section", "shard", None),
        P(),
        P(),
    )
    return jax.shard_map(
        per_device,
        mesh=mesh,
        in_specs=placed,
        out_specs=(
            P("replica", "section", None, "shard"),
            P("replica", "section", "shard", None),
            P("replica", "section", None, "shard"),
            P("replica", "section", "shard", None),
        ),
        check_vma=False,
    )
```

```python
import functools
import math

import jax
import jax.numpy as jnp
from jax import lax
from jax.experimental import pallas as pl
from jax.experimental.pallas import tpu as pltpu
from jax.sharding import PartitionSpec as P

MESH = pl.DeviceIdType.MESH
f32 = jnp.float32
bf16 = jnp.bfloat16

epsilon = 1e-05
inner_rate = 0.5
momentum_decay = 0.9
outer_rate = 0.7

step_size = outer_rate * (1.0 + momentum_decay)
mix_rate = step_size * momentum_decay - outer_rate * momentum_decay * momentum_decay

REPLICAS = 16
SECTIONS = 4
SHARDS = 4
ROWS = 128
GROUP = ROWS // REPLICAS
WIDTH = 1024
FEATURES = WIDTH // SHARDS
HIDDEN = 768
PIECE_A = WIDTH // REPLICAS
PIECE_B = HIDDEN // REPLICAS
scale_in = 1.0 / math.sqrt(WIDTH)
scale_out = 1.0 / math.sqrt(HIDDEN * SHARDS)

RELAYED_B = (15, 14)
RELAYED_A = (15,)

NN = (((1,), (0,)), ((), ()))
NT = (((1,), (1,)), ((), ()))


def dot(a, b, dims=NN):
    return lax.dot_general(a, b, dims, preferred_element_type=f32)


def pack_rows(wide):
    return jnp.concatenate([wide[:, :, :128], wide[:, :, 128:]], axis=1).astype(bf16)


def unpack_rows(packed):
    wide = packed.astype(f32)
    count = wide.shape[0]
    return jnp.concatenate(
        [
            wide[:, :GROUP, :].reshape(count * GROUP, 128),
            wide[:, GROUP:, :].reshape(count * GROUP, 128),
        ],
        axis=1,
    )


def kernel(
    inp_h, tgt_h, wa_h, wb_h, ma_h, mb_h, routes, partners,
    new_wa, new_wb, new_ma, new_mb,
    inp, tgt, wa, wb, ma, mb,
    fwd_all, fwd_term, fwd_got, fwd_out, fwd_send, fwd_recv,
    bwd_all, bwd_term, bwd_got, bwd_send, bwd_recv, along_send, along_got, up_own,
    inv_rms, slope, hidden_t, normed_t, grad_pre, grad_a, grad_b,
    qa_send, qb_send, qa_recv, qb_recv, va_send, vb_send, va_recv, vb_recv,
    order_f, order_a, order_b,
    load_sem, x_send, x_recv, z_send, z_recv, bulk_send, bulk_recv,
    relay_b, relay_a, relay_send, relay_recv,
):
    r = lax.axis_index("replica")
    s = lax.axis_index("section")
    x = lax.axis_index("shard")
    y, z = r // 8, lax.rem(r, 8)
    across = (1 - y) * 8 + z
    first, last = s == 0, s == SECTIONS - 1

    def other_shard(d):
        return lax.rem(x + d, SHARDS)

    def peer(t):
        dy, h = lax.rem(t, 2), t // 2
        odd = lax.rem(h, 2)
        dz = odd * ((h + 1) // 2) + (1 - odd) * lax.rem(8 - h // 2, 8)
        return lax.rem(y + dy, 2) * 8 + lax.rem(z + dz, 8)

    def each(count, body, start=0):
        def step(i, carry):
            body(i)
            return carry

        lax.fori_loop(start, count, step, 0)

    loads = [
        pltpu.make_async_copy(src, dst, load_sem.at[i])
        for i, (src, dst) in enumerate(
            [(inp_h, inp), (wa_h, wa), (wb_h, wb), (ma_h, ma), (mb_h, mb), (tgt_h, tgt)]
        )
    ]
    for copy in loads:
        copy.start()

    barrier = pltpu.get_barrier_semaphore()

    def greet(device):
        pl.semaphore_signal(barrier, inc=1, device_id=device, device_id_type=MESH)

    for d in (1, 2, 3):
        greet((r, s, other_shard(d)))

    @pl.when(s < SECTIONS - 1)
    def _():
        each(REPLICAS, lambda t: greet((peer(t), s + 1, x)))

    @pl.when(s > 0)
    def _():
        each(REPLICAS, lambda t: greet((peer(t), s - 1, x)))

    each(REPLICAS, lambda t: greet((peer(t), s, x)), 1)

    @pl.when(s >= 2)
    def _():
        greet((across, s - 2, x))

    @pl.when(s < 2)
    def _():
        greet((lax.rem(z + 4, 8), s + 2, x))
        greet((8 + lax.rem(z + 4, 8), s + 2, x))

    links = jnp.minimum(s, 1) + jnp.minimum(SECTIONS - 1 - s, 1)
    pl.semaphore_wait(barrier, SHARDS - 1 + REPLICAS - 1 + REPLICAS * links + 1 + s // 2)


    def gather_copy(ref, phase, d):
        return pltpu.make_async_remote_copy(
            ref.at[x], ref.at[x], x_send.at[phase, d], x_recv.at[phase, d],
            device_id=(r, s, other_shard(d)), device_id_type=MESH,
        )

    def scatter_copy(src, dst, phase, d):
        return pltpu.make_async_remote_copy(
            src.at[other_shard(d)], dst.at[x], x_send.at[phase, d], x_recv.at[phase, d],
            device_id=(r, s, other_shard(d)), device_id_type=MESH,
        )

    def route_copy(src, slot, dst, phase, t, section):
        return pltpu.make_async_remote_copy(
            src.at[slot], dst.at[r], z_send.at[phase], z_recv.at[phase],
            device_id=(peer(t), section, x), device_id_type=MESH,
        )

    def route_wait_recv(dst, phase):
        pltpu.make_async_copy(dst, dst, z_recv.at[phase]).wait()

    def route_wait_send(src, phase):
        pltpu.make_async_copy(src, src, z_send.at[phase]).wait()

    def bulk_start(src, dst, which, count=REPLICAS):
        def body(t):
            p = peer(t)
            pltpu.make_async_remote_copy(
                src.at[p], dst.at[r], bulk_send.at[which], bulk_recv.at[which],
                device_id=(p, s, x), device_id_type=MESH,
            ).start()

        each(count, body, 1)

    def late_start(src, dst, which, buffer, relayed):
        @pl.when(s < 2)
        def _():
            for i, t in enumerate(relayed):
                pltpu.make_async_remote_copy(
                    src.at[peer(t)], buffer.at[i], bulk_send.at[which], relay_recv.at[which - 2],
                    device_id=(across, s + 2, x), device_id_type=MESH,
                ).start()

        bulk_start(src, dst, which, REPLICAS - len(relayed) * jnp.maximum(1 - s // 2, 0))

    def relay(dst, which, buffer, relayed):
        pltpu.make_async_copy(buffer, buffer, relay_recv.at[which - 2]).wait()
        for i, t in enumerate(relayed):
            pltpu.make_async_remote_copy(
                buffer.at[i], dst.at[across], relay_send.at[which - 2], bulk_recv.at[which],
                device_id=(lax.rem(1 - y + t % 2, 2) * 8 + lax.rem(z + 4, 8), s - 2, x),
                device_id_type=MESH,
            ).start()

    def bulk_wait_recv(dst, which):
        part = dst.at[0 : REPLICAS - 1]
        pltpu.make_async_copy(part, part, bulk_recv.at[which]).wait()

    def bulk_wait_send(src, which):
        part = src.at[0 : REPLICAS - 1]
        pltpu.make_async_copy(part, part, bulk_send.at[which]).wait()


    def invert(table, out):
        def body(p):
            found = 0
            for g in range(REPLICAS):
                apart = table(g) - p
                found = jnp.maximum(found, g * (1 - jnp.minimum(apart * apart, 1)))
            out[p] = found

        each(REPLICAS, body)

    link = jnp.minimum(s, SECTIONS - 2)


    def fill_q(w, m, order, send, recv):
        def body(p):
            k = order[p]
            value = (w[k].astype(f32) + mix_rate * m[k].astype(f32)).astype(bf16)
            send[p] = value

        each(REPLICAS, body)
        recv[r] = send[r]

    def fill_v(m, grad, factor, order, send, recv):
        def body(p):
            k = order[p]
            value = momentum_decay * m[k].astype(f32) + factor * grad[k]
            send[p] = value.astype(bf16)

        each(REPLICAS, body)
        recv[r] = send[r]

    def prepare_q():
        invert(lambda g: partners[s, 0, g, r], order_a)
        invert(lambda g: partners[s, 1, g, r], order_b)
        loads[3].wait()
        loads[4].wait()
        fill_q(wb, mb, order_b, qb_send, qb_recv)
        fill_q(wa, ma, order_a, qa_send, qa_recv)

    def rows_a(j):
        span = FEATURES // PIECE_A
        return wa[pl.ds(j * span, span)].reshape(FEATURES, HIDDEN)

    def columns_b(j):
        columns = pl.ds(pl.multiple_of(j * FEATURES, FEATURES), FEATURES)
        return wb[:, :, columns].reshape(HIDDEN, FEATURES)


    loads[0].wait()

    @pl.when(first)
    def _():
        fwd_all[x] = inp[...]

    @pl.when(s > 0)
    def _():
        loads[1].wait()
        loads[2].wait()
        prepare_q()

    @pl.when(s >= 2)
    def _():
        bulk_start(qb_send, qb_recv, 0)

    @pl.when(last)
    def _():
        bulk_start(qa_send, qa_recv, 1)

    @pl.when(s > 0)
    def _():
        invert(lambda g: routes[link, r, g], order_f)
        route_wait_recv(fwd_recv, 0)
        fwd_all[x] = unpack_rows(fwd_recv[...]).astype(bf16)

    for d in (2, 1, 3):
        gather_copy(fwd_all, 0, d).start()

    @pl.when(first)
    def _():
        invert(lambda g: routes[link, r, g], order_f)
        loads[1].wait()
        loads[2].wait()

    preact = jnp.zeros((ROWS, HIDDEN), f32)
    square = jnp.zeros((ROWS, 1), f32)
    for d in (0, 1, 3, 2):
        if d:
            gather_copy(fwd_all, 0, d).wait_recv()
        j = lax.rem(x + SHARDS - d, SHARDS)
        part = fwd_all[j]
        preact = preact + dot(part, rows_a(j))
        wide = part.astype(f32)
        square = square + jnp.sum(wide * wide, axis=1, keepdims=True)
    inverse = lax.rsqrt(square * (1.0 / WIDTH) + epsilon)
    inv_rms[...] = jnp.broadcast_to(inverse, inv_rms.shape)
    preact = preact * (inverse * scale_in)
    gate = 1.0 / (1.0 + jnp.exp(-preact))
    hidden = (preact * gate).astype(bf16)
    slope[...] = (gate * (1.0 + preact * (1.0 - gate))) * scale_out
    for d in (2, 1, 3, 0):
        j = other_shard(d)
        fwd_term[j] = (dot(hidden, columns_b(j)) * scale_out).astype(bf16)
        if d:
            scatter_copy(fwd_term, fwd_got, 1, d).start()
    total = fwd_term[x].astype(f32)
    for d in (1, 3, 2):
        scatter_copy(fwd_term, fwd_got, 1, d).wait_recv()
        total = total + fwd_got[lax.rem(x + SHARDS - d, SHARDS)].astype(f32)
    output = (fwd_all[x].astype(f32) + total).astype(bf16).astype(f32)

    @pl.when(s < SECTIONS - 1)
    def _():
        fwd_out[...] = output.reshape(REPLICAS, GROUP, FEATURES)
        for t in range(REPLICAS - 1, -1, -1):
            block = fwd_out[order_f[peer(t)]]
            fwd_send[t] = pack_rows(block[None])[0]
            route_copy(fwd_send, t, fwd_recv, 0, t, s + 1).start()

    @pl.when(last)
    def _():
        loads[5].wait()
        up = (output - tgt[...].astype(f32)).astype(bf16)
        bwd_all[x] = up
        up_own[...] = up.astype(f32)
        for d in (2, 1, 3):
            gather_copy(bwd_all, 2, d).start()


    @pl.when(first)
    def _():
        prepare_q()
        bulk_start(qb_send, qb_recv, 0)

    @pl.when(s == 1)
    def _():
        bulk_start(qb_send, qb_recv, 0)

    @pl.when(s < SECTIONS - 1)
    def _():
        loads[5].wait()
        bulk_start(qa_send, qa_recv, 1)

    hidden_t[...] = hidden.T
    for j in range(SHARDS):
        normed = (fwd_all[j].astype(f32) * inverse).astype(bf16)
        normed_t[j * FEATURES : (j + 1) * FEATURES, :] = normed.T


    @pl.when(s < SECTIONS - 1)
    def _():
        route_wait_recv(bwd_recv, 1)
        for g in range(REPLICAS):
            block = bwd_recv[routes[link, r, g]]
            up_own[g * GROUP : (g + 1) * GROUP, :] = unpack_rows(block[None])
        bwd_all[x] = up_own[...].astype(bf16)
        for d in (2, 1, 3):
            gather_copy(bwd_all, 2, d).start()

    grad_hidden = jnp.zeros((ROWS, HIDDEN), f32)
    for d in (0, 1, 3, 2):
        if d:
            gather_copy(bwd_all, 2, d).wait_recv()
        j = lax.rem(x + SHARDS - d, SHARDS)
        grad_hidden = grad_hidden + dot(bwd_all[j], columns_b(j), NT)
    grad_pre[...] = (grad_hidden * slope[...]).astype(bf16)

    def outer_b():
        for j in range(SHARDS):
            value = dot(hidden_t[...], bwd_all[j]).reshape(REPLICAS, PIECE_B, FEATURES)
            grad_b[:, :, j * FEATURES : (j + 1) * FEATURES] = value
        fill_v(mb, grad_b, inner_rate * scale_out, order_b, vb_send, vb_recv)
        late_start(vb_send, vb_recv, 2, relay_b, RELAYED_B)

    def outer_a():
        for j in range(SHARDS):
            value = dot(normed_t[j * FEATURES : (j + 1) * FEATURES, :], grad_pre[...])
            span = FEATURES // PIECE_A
            grad_a[j * span : (j + 1) * span] = value.reshape(span, PIECE_A, HIDDEN)
        fill_v(ma, grad_a, inner_rate * scale_in, order_a, va_send, va_recv)
        late_start(va_send, va_recv, 3, relay_a, RELAYED_A)

    @pl.when(s <= 1)
    def _():
        outer_b()

    @pl.when(s > 0)
    def _():
        inverse = inv_rms[:, :1]
        share = jnp.zeros((ROWS, 1), f32)
        for d in (2, 1, 3, 0):
            j = other_shard(d)
            term = (dot(grad_pre[...], rows_a(j), NT) * scale_in).astype(bf16)
            bwd_term[j] = term
            if d:
                scatter_copy(bwd_term, bwd_got, 3, d).start()
            exact = fwd_all[j].astype(f32) * inverse
            share = share + jnp.sum(term.astype(f32) * exact, axis=1, keepdims=True)
        diagonal = lax.broadcasted_iota(jnp.int32, (ROWS, ROWS), 0) == lax.broadcasted_iota(
            jnp.int32, (ROWS, ROWS), 1
        )
        row = jnp.sum(jnp.where(diagonal, share, 0.0), axis=0, keepdims=True)
        along_send[...] = jnp.broadcast_to(row, along_send.shape)

        def along_copy(d):
            return pltpu.make_async_remote_copy(
                along_send, along_got.at[x], x_send.at[4, d], x_recv.at[4, d],
                device_id=(r, s, other_shard(d)), device_id_type=MESH,
            )

        for d in (2, 1, 3):
            along_copy(d).start()
        total = bwd_term[x].astype(f32)
        for d in (1, 3, 2):
            scatter_copy(bwd_term, bwd_got, 3, d).wait_recv()
            total = total + bwd_got[lax.rem(x + SHARDS - d, SHARDS)].astype(f32)
        for d in (1, 3, 2):
            along_copy(d).wait_recv()
            row = row + along_got[lax.rem(x + SHARDS - d, SHARDS)][:1, :]
        along = jnp.sum(jnp.where(diagonal, row, 0.0), axis=1, keepdims=True) * (1.0 / WIDTH)
        exact = fwd_all[x].astype(f32) * inverse
        result = up_own[...] + inverse * (total - exact * along)
        bwd_send[...] = pack_rows(result.reshape(REPLICAS, GROUP, FEATURES))
        for t in range(REPLICAS - 1, -1, -1):
            route_copy(bwd_send, peer(t), bwd_recv, 1, t, s - 1).start()
        for d in (1, 3, 2):
            scatter_copy(bwd_term, bwd_got, 3, d).wait_send()
            along_copy(d).wait_send()

    @pl.when(s > 1)
    def _():
        outer_b()

    outer_a()

    @pl.when(s >= 2)
    def _():
        relay(vb_recv, 2, relay_b, RELAYED_B)
        relay(va_recv, 3, relay_a, RELAYED_A)


    def outer_step(w, m, grad, factor, table, q_recv, v_recv, new_w, new_m):
        def body(k):
            partner = partners[s, table, k, r]
            weight = w[k].astype(f32)
            moment = m[k].astype(f32)
            own = momentum_decay * moment + factor * grad[k]
            new_moment = 0.5 * (own + v_recv[partner].astype(f32))
            kept = 0.5 * (weight + mix_rate * moment + q_recv[partner].astype(f32))
            new_w[k] = (kept - step_size * new_moment).astype(bf16)
            new_m[k] = new_moment.astype(bf16)

        each(REPLICAS, body)

    bulk_wait_recv(qb_recv, 0)
    bulk_wait_recv(vb_recv, 2)
    outer_step(wb, mb, grad_b, inner_rate * scale_out, 1, qb_recv, vb_recv, new_wb, new_mb)
    bulk_wait_recv(qa_recv, 1)
    bulk_wait_recv(va_recv, 3)
    outer_step(wa, ma, grad_a, inner_rate * scale_in, 0, qa_recv, va_recv, new_wa, new_ma)

    for d in (1, 2, 3):
        gather_copy(fwd_all, 0, d).wait_send()
        scatter_copy(fwd_term, fwd_got, 1, d).wait_send()
        gather_copy(bwd_all, 2, d).wait_send()

    @pl.when(s < SECTIONS - 1)
    def _():
        route_wait_send(fwd_send, 0)

    @pl.when(s > 0)
    def _():
        route_wait_send(bwd_send, 1)

    @pl.when(s >= 2)
    def _():
        pltpu.make_async_copy(relay_b, relay_b, relay_send.at[0]).wait()
        pltpu.make_async_copy(relay_a, relay_a, relay_send.at[1]).wait()

    for which, src in enumerate((qb_send, qa_send, vb_send, va_send)):
        bulk_wait_send(src, which)


def per_device(inputs, targets, weight_a, weight_b, moment_a, moment_b, routes, partners):
    def vmem(*shape, dtype=bf16):
        return pltpu.VMEM(shape, dtype)

    shards = (SHARDS, ROWS, FEATURES)
    routed = (REPLICAS, 2 * GROUP, 128)
    bulk_a = (REPLICAS, PIECE_A, HIDDEN)
    bulk_b = (REPLICAS, PIECE_B, WIDTH)
    dma = pltpu.SemaphoreType.DMA
    shape_a = pltpu.VMEM(bulk_a, bf16)
    shape_b = pltpu.VMEM(bulk_b, bf16)
    far = pl.BlockSpec(memory_space=pltpu.HBM)
    smem = pl.BlockSpec(memory_space=pltpu.SMEM)
    new_wa, new_wb, new_ma, new_mb = pl.pallas_call(
        kernel,
        out_shape=(shape_a, shape_b, shape_a, shape_b),
        in_specs=[far] * 6 + [smem, smem],
        out_specs=(pl.BlockSpec(memory_space=pltpu.VMEM),) * 4,
        scratch_shapes=[
            vmem(ROWS, FEATURES), vmem(ROWS, FEATURES),
            vmem(*bulk_a), vmem(*bulk_b), vmem(*bulk_a), vmem(*bulk_b),
            vmem(*shards), vmem(*shards), vmem(*shards), vmem(REPLICAS, GROUP, FEATURES, dtype=f32),
            vmem(*routed), vmem(*routed),
            vmem(*shards), vmem(*shards), vmem(*shards), vmem(*routed), vmem(*routed),
            vmem(8, ROWS, dtype=f32), vmem(SHARDS, 8, ROWS, dtype=f32),
            vmem(ROWS, FEATURES, dtype=f32),
            vmem(ROWS, 128, dtype=f32), vmem(ROWS, HIDDEN, dtype=f32),
            vmem(HIDDEN, ROWS), vmem(WIDTH, ROWS), vmem(ROWS, HIDDEN),
            vmem(*bulk_a, dtype=f32), vmem(*bulk_b, dtype=f32),
            vmem(*bulk_a), vmem(*bulk_b), vmem(*bulk_a), vmem(*bulk_b),
            vmem(*bulk_a), vmem(*bulk_b), vmem(*bulk_a), vmem(*bulk_b),
            pltpu.SMEM((REPLICAS,), jnp.int32), pltpu.SMEM((REPLICAS,), jnp.int32),
            pltpu.SMEM((REPLICAS,), jnp.int32),
            dma((6,)), dma((5, SHARDS)), dma((5, SHARDS)), dma((2,)), dma((2,)),
            dma((4,)), dma((4,)),
            vmem(len(RELAYED_B), PIECE_B, WIDTH), vmem(len(RELAYED_A), PIECE_A, HIDDEN),
            dma((2,)), dma((2,)),
        ],
        compiler_params=pltpu.CompilerParams(
            collective_id=0, has_side_effects=True, vmem_limit_bytes=56 * 2**20
        ),
    )(
        inputs[0, 0], targets[0, 0], weight_a.reshape(bulk_a), weight_b.reshape(bulk_b),
        moment_a.reshape(bulk_a), moment_b.reshape(bulk_b), routes[0], partners,
    )
    return (
        new_wa.reshape(weight_a.shape), new_wb.reshape(weight_b.shape),
        new_ma.reshape(moment_a.shape), new_mb.reshape(moment_b.shape),
    )


def solution(mesh):
    placed = (
        P("replica", None, None, "shard"),
        P("replica", None, None, "shard"),
        P("replica", "section", None, "shard"),
        P("replica", "section", "shard", None),
        P("replica", "section", None, "shard"),
        P("replica", "section", "shard", None),
        P(),
        P(),
    )
    return jax.shard_map(
        per_device,
        mesh=mesh,
        in_specs=placed,
        out_specs=(
            P("replica", "section", None, "shard"),
            P("replica", "section", "shard", None),
            P("replica", "section", None, "shard"),
            P("replica", "section", "shard", None),
        ),
        check_vma=False,
    )
```

```python
import functools
import math

import jax
import jax.numpy as jnp
from jax import lax
from jax.experimental import pallas as pl
from jax.experimental.pallas import tpu as pltpu
from jax.sharding import PartitionSpec as P

MESH = pl.DeviceIdType.MESH
f32 = jnp.float32
bf16 = jnp.bfloat16

epsilon = 1e-05
inner_rate = 0.5
momentum_decay = 0.9
outer_rate = 0.7

step_size = outer_rate * (1.0 + momentum_decay)
mix_rate = step_size * momentum_decay - outer_rate * momentum_decay * momentum_decay

REPLICAS = 16
SECTIONS = 4
SHARDS = 4
ROWS = 128
GROUP = ROWS // REPLICAS
WIDTH = 1024
FEATURES = WIDTH // SHARDS
HIDDEN = 768
PIECE_A = WIDTH // REPLICAS
PIECE_B = HIDDEN // REPLICAS
scale_in = 1.0 / math.sqrt(WIDTH)
scale_out = 1.0 / math.sqrt(HIDDEN * SHARDS)

EARLY_B = (15,)
EARLY_A = (15,)
LATE_B = (15, 14)
LATE_A = (15,)
FIRST_Q = 7

NN = (((1,), (0,)), ((), ()))
NT = (((1,), (1,)), ((), ()))


def dot(a, b, dims=NN):
    return lax.dot_general(a, b, dims, preferred_element_type=f32)


def pack_rows(wide):
    return jnp.concatenate([wide[:, :, :128], wide[:, :, 128:]], axis=1).astype(bf16)


def unpack_rows(packed):
    wide = packed.astype(f32)
    count = wide.shape[0]
    return jnp.concatenate(
        [
            wide[:, :GROUP, :].reshape(count * GROUP, 128),
            wide[:, GROUP:, :].reshape(count * GROUP, 128),
        ],
        axis=1,
    )


def kernel(
    inp_h, tgt_h, wa_h, wb_h, ma_h, mb_h, routes, partners,
    new_wa, new_wb, new_ma, new_mb,
    inp, tgt, wa, wb, ma, mb,
    fwd_all, fwd_term, fwd_got, fwd_out, fwd_send, fwd_recv,
    bwd_all, bwd_term, bwd_got, bwd_send, bwd_recv, along_send, along_got, up_own,
    inv_rms, slope, hidden_t, normed_t, grad_pre, grad_a, grad_b,
    qa_send, qb_send, qa_recv, qb_recv, va_send, vb_send, va_recv, vb_recv,
    order_f, order_a, order_b,
    load_sem, x_send, x_recv, z_send, z_recv, bulk_send, bulk_recv,
    relay_b, relay_a, relay_send, relay_recv, clear,
):
    r = lax.axis_index("replica")
    s = lax.axis_index("section")
    x = lax.axis_index("shard")
    y, z = r // 8, lax.rem(r, 8)
    across = (1 - y) * 8 + z
    first, last = s == 0, s == SECTIONS - 1

    def other_shard(d):
        return lax.rem(x + d, SHARDS)

    def peer(t):
        dy, h = lax.rem(t, 2), t // 2
        odd = lax.rem(h, 2)
        dz = odd * ((h + 1) // 2) + (1 - odd) * lax.rem(8 - h // 2, 8)
        return lax.rem(y + dy, 2) * 8 + lax.rem(z + dz, 8)

    def each(count, body, start=0):
        def step(i, carry):
            body(i)
            return carry

        lax.fori_loop(start, count, step, 0)

    loads = [
        pltpu.make_async_copy(src, dst, load_sem.at[i])
        for i, (src, dst) in enumerate(
            [(inp_h, inp), (wa_h, wa), (wb_h, wb), (ma_h, ma), (mb_h, mb), (tgt_h, tgt)]
        )
    ]
    for copy in loads:
        copy.start()

    barrier = pltpu.get_barrier_semaphore()

    def greet(device):
        pl.semaphore_signal(barrier, inc=1, device_id=device, device_id_type=MESH)

    for d in (1, 2, 3):
        greet((r, s, other_shard(d)))

    @pl.when(s < SECTIONS - 1)
    def _():
        each(REPLICAS, lambda t: greet((peer(t), s + 1, x)))

    @pl.when(s > 0)
    def _():
        each(REPLICAS, lambda t: greet((peer(t), s - 1, x)))

    each(REPLICAS, lambda t: greet((peer(t), s, x)), 1)

    other = lax.rem(s + 2, SECTIONS)
    greet((across, other, x))
    greet((lax.rem(z + 4, 8), other, x))
    greet((8 + lax.rem(z + 4, 8), other, x))


    def invert(table, out):
        def body(p):
            found = 0
            for g in range(REPLICAS):
                apart = table(g) - p
                found = jnp.maximum(found, g * (1 - jnp.minimum(apart * apart, 1)))
            out[p] = found

        each(REPLICAS, body)

    link = jnp.minimum(s, SECTIONS - 2)


    def fill_q(w, m, order, send, recv):
        def body(p):
            k = order[p]
            value = (w[k].astype(f32) + mix_rate * m[k].astype(f32)).astype(bf16)
            send[p] = value

        each(REPLICAS, body)
        recv[r] = send[r]

    def make_v(m, grad, factor, order, send):
        def body(p):
            k = order[p]
            value = momentum_decay * m[k].astype(f32) + factor * grad[k]
            send[p] = value.astype(bf16)

        return body

    def prepare_q(needed):
        invert(lambda g: partners[s, 0, g, r], order_a)
        invert(lambda g: partners[s, 1, g, r], order_b)
        for i in needed:
            loads[i].wait()
        fill_q(wb, mb, order_b, qb_send, qb_recv)
        fill_q(wa, ma, order_a, qa_send, qa_recv)

    @pl.when(s > 0)
    def _():
        prepare_q((2, 4, 1, 3))

    links = jnp.minimum(s, 1) + jnp.minimum(SECTIONS - 1 - s, 1)
    pl.semaphore_wait(barrier, SHARDS - 1 + REPLICAS - 1 + REPLICAS * links + 3)


    def gather_copy(ref, phase, d):
        return pltpu.make_async_remote_copy(
            ref.at[x], ref.at[x], x_send.at[phase, d], x_recv.at[phase, d],
            device_id=(r, s, other_shard(d)), device_id_type=MESH,
        )

    def scatter_copy(src, dst, phase, d):
        return pltpu.make_async_remote_copy(
            src.at[other_shard(d)], dst.at[x], x_send.at[phase, d], x_recv.at[phase, d],
            device_id=(r, s, other_shard(d)), device_id_type=MESH,
        )

    def route_copy(src, slot, dst, phase, t, section):
        return pltpu.make_async_remote_copy(
            src.at[slot], dst.at[r], z_send.at[phase], z_recv.at[phase],
            device_id=(peer(t), section, x), device_id_type=MESH,
        )

    def route_wait_recv(dst, phase):
        pltpu.make_async_copy(dst, dst, z_recv.at[phase]).wait()

    def route_wait_send(src, phase):
        pltpu.make_async_copy(src, src, z_send.at[phase]).wait()

    def bulk_start(src, dst, which, count=REPLICAS, make=None, skip=0, stop=None):
        def body(t):
            p = peer(t)
            if make is not None:
                make(p)
            pltpu.make_async_remote_copy(
                src.at[p], dst.at[r], bulk_send.at[which], bulk_recv.at[which],
                device_id=(p, s, x), device_id_type=MESH,
            ).start()

        each(count - 1 if stop is None else stop, lambda i: body(count - 1 - i), skip)

    def detour_start(src, which, buffer, relayed, section, make=None):
        for i, t in enumerate(relayed):
            if make is not None:
                make(peer(t))
            pltpu.make_async_remote_copy(
                src.at[peer(t)], buffer.at[i], bulk_send.at[which], relay_recv.at[which],
                device_id=(across, section, x), device_id_type=MESH,
            ).start()

    def relay(dst, which, buffer, relayed, section):
        if not relayed:
            return
        part = buffer.at[0 : len(relayed)]
        pltpu.make_async_copy(part, part, relay_recv.at[which]).wait()
        for i, t in enumerate(relayed):
            pltpu.make_async_remote_copy(
                buffer.at[i], dst.at[across], relay_send.at[which], bulk_recv.at[which],
                device_id=(lax.rem(1 - y + t % 2, 2) * 8 + lax.rem(z + 4, 8), section, x),
                device_id_type=MESH,
            ).start()

    def relay_wait_send(which, buffer, relayed):
        if not relayed:
            return
        part = buffer.at[0 : len(relayed)]
        pltpu.make_async_copy(part, part, relay_send.at[which]).wait()

    def direct(relayed, upper):
        return REPLICAS - len(relayed) * (s // 2 if upper else 1 - s // 2)

    def bulk_wait_recv(dst, which):
        part = dst.at[0 : REPLICAS - 1]
        pltpu.make_async_copy(part, part, bulk_recv.at[which]).wait()

    def bulk_wait_send(src, which):
        part = src.at[0 : REPLICAS - 1]
        pltpu.make_async_copy(part, part, bulk_send.at[which]).wait()

    def rows_a(j):
        span = FEATURES // PIECE_A
        return wa[pl.ds(j * span, span)].reshape(FEATURES, HIDDEN)

    def columns_b(j):
        columns = pl.ds(pl.multiple_of(j * FEATURES, FEATURES), FEATURES)
        return wb[:, :, columns].reshape(HIDDEN, FEATURES)


    loads[0].wait()

    @pl.when(first)
    def _():
        fwd_all[x] = inp[...]

    @pl.when(s > 0)
    def _():
        loads[5].wait()

    @pl.when(s >= 2)
    def _():
        detour_start(qb_send, 0, relay_b, EARLY_B, s - 2)
        detour_start(qa_send, 1, relay_a, EARLY_A, s - 2)
        bulk_start(qb_send, qb_recv, 0, direct(EARLY_B, True))

    @pl.when(last)
    def _():
        bulk_start(qa_send, qa_recv, 1, direct(EARLY_A, True))

    def relay_q():
        relay(qb_recv, 0, relay_b, EARLY_B, s + 2)
        relay(qa_recv, 1, relay_a, EARLY_A, s + 2)

    @pl.when(s > 0)
    def _():
        invert(lambda g: routes[link, r, g], order_f)
        route_wait_recv(fwd_recv, 0)
        fwd_all[x] = unpack_rows(fwd_recv[...]).astype(bf16)

    for d in (2, 1, 3):
        gather_copy(fwd_all, 0, d).start()

    @pl.when(first)
    def _():
        invert(lambda g: routes[link, r, g], order_f)
        loads[1].wait()
        loads[2].wait()
        loads[5].wait()

    preact = jnp.zeros((ROWS, HIDDEN), f32)
    square = jnp.zeros((ROWS, 1), f32)
    for d in (0, 1, 3, 2):
        if d:
            gather_copy(fwd_all, 0, d).wait_recv()
        j = lax.rem(x + SHARDS - d, SHARDS)
        part = fwd_all[j]
        preact = preact + dot(part, rows_a(j))
        wide = part.astype(f32)
        square = square + jnp.sum(wide * wide, axis=1, keepdims=True)
    inverse = lax.rsqrt(square * (1.0 / WIDTH) + epsilon)
    inv_rms[...] = jnp.broadcast_to(inverse, inv_rms.shape)
    preact = preact * (inverse * scale_in)
    gate = 1.0 / (1.0 + jnp.exp(-preact))
    hidden = (preact * gate).astype(bf16)
    for d in (2, 1, 3, 0):
        j = other_shard(d)
        fwd_term[j] = (dot(hidden, columns_b(j)) * scale_out).astype(bf16)
        if d:
            scatter_copy(fwd_term, fwd_got, 1, d).start()
    slope[...] = (gate * (1.0 + preact * (1.0 - gate))) * scale_out
    total = fwd_term[x].astype(f32)
    for d in (1, 3, 2):
        scatter_copy(fwd_term, fwd_got, 1, d).wait_recv()
        total = total + fwd_got[lax.rem(x + SHARDS - d, SHARDS)].astype(f32)
    output = (fwd_all[x].astype(f32) + total).astype(bf16).astype(f32)

    @pl.when(s < SECTIONS - 1)
    def _():
        fwd_out[...] = output.reshape(REPLICAS, GROUP, FEATURES)
        for t in range(REPLICAS - 1, -1, -1):
            block = fwd_out[order_f[peer(t)]]
            fwd_send[t] = pack_rows(block[None])[0]
            route_copy(fwd_send, t, fwd_recv, 0, t, s + 1).start()

    @pl.when(last)
    def _():
        up = (output - tgt[...].astype(f32)).astype(bf16)
        bwd_all[x] = up
        up_own[...] = up.astype(f32)
        for d in (2, 1, 3):
            gather_copy(bwd_all, 2, d).start()


    @pl.when(first)
    def _():
        prepare_q((3, 4))
        bulk_start(qb_send, qb_recv, 0, stop=FIRST_Q)
        pl.semaphore_wait(clear, 1)
        bulk_start(qb_send, qb_recv, 0, skip=FIRST_Q)

    @pl.when(s == 1)
    def _():
        pl.semaphore_signal(clear, inc=1, device_id=(r, 0, x), device_id_type=MESH)
        bulk_start(qb_send, qb_recv, 0)

    @pl.when(s < SECTIONS - 1)
    def _():
        bulk_start(qa_send, qa_recv, 1, direct(EARLY_A, True))

    @pl.when(s < 2)
    def _():
        relay_q()

    hidden_t[...] = hidden.T
    for j in range(SHARDS):
        normed = (fwd_all[j].astype(f32) * inverse).astype(bf16)
        normed_t[j * FEATURES : (j + 1) * FEATURES, :] = normed.T


    @pl.when(s < SECTIONS - 1)
    def _():
        route_wait_recv(bwd_recv, 1)
        for g in range(REPLICAS):
            block = bwd_recv[routes[link, r, g]]
            up_own[g * GROUP : (g + 1) * GROUP, :] = unpack_rows(block[None])
        bwd_all[x] = up_own[...].astype(bf16)
        for d in (2, 1, 3):
            gather_copy(bwd_all, 2, d).start()

    grad_hidden = jnp.zeros((ROWS, HIDDEN), f32)
    for d in (0, 1, 3, 2):
        if d:
            gather_copy(bwd_all, 2, d).wait_recv()
        j = lax.rem(x + SHARDS - d, SHARDS)
        grad_hidden = grad_hidden + dot(bwd_all[j], columns_b(j), NT)
    grad_pre[...] = (grad_hidden * slope[...]).astype(bf16)

    def outer_b():
        for j in range(SHARDS):
            value = dot(hidden_t[...], bwd_all[j]).reshape(REPLICAS, PIECE_B, FEATURES)
            grad_b[:, :, j * FEATURES : (j + 1) * FEATURES] = value
        make = make_v(mb, grad_b, inner_rate * scale_out, order_b, vb_send)
        @pl.when(s < 2)
        def _():
            detour_start(vb_send, 2, relay_b, LATE_B, s + 2, make)

        bulk_start(vb_send, vb_recv, 2, direct(LATE_B, False), make)
        make(r)
        vb_recv[r] = vb_send[r]

    def outer_a():
        for j in range(SHARDS):
            value = dot(normed_t[j * FEATURES : (j + 1) * FEATURES, :], grad_pre[...])
            span = FEATURES // PIECE_A
            grad_a[j * span : (j + 1) * span] = value.reshape(span, PIECE_A, HIDDEN)
        make = make_v(ma, grad_a, inner_rate * scale_in, order_a, va_send)

        @pl.when(s < 2)
        def _():
            detour_start(va_send, 3, relay_a, LATE_A, s + 2, make)

        bulk_start(va_send, va_recv, 3, direct(LATE_A, False), make)
        make(r)
        va_recv[r] = va_send[r]

    @pl.when(s <= 1)
    def _():
        outer_b()

    @pl.when(s > 0)
    def _():
        inverse = inv_rms[:, :1]
        share = jnp.zeros((ROWS, 1), f32)
        for d in (2, 1, 3, 0):
            j = other_shard(d)
            term = (dot(grad_pre[...], rows_a(j), NT) * scale_in).astype(bf16)
            bwd_term[j] = term
            if d:
                scatter_copy(bwd_term, bwd_got, 3, d).start()
            exact = fwd_all[j].astype(f32) * inverse
            share = share + jnp.sum(term.astype(f32) * exact, axis=1, keepdims=True)
        diagonal = lax.broadcasted_iota(jnp.int32, (ROWS, ROWS), 0) == lax.broadcasted_iota(
            jnp.int32, (ROWS, ROWS), 1
        )
        row = jnp.sum(jnp.where(diagonal, share, 0.0), axis=0, keepdims=True)
        along_send[...] = jnp.broadcast_to(row, along_send.shape)

        def along_copy(d):
            return pltpu.make_async_remote_copy(
                along_send, along_got.at[x], x_send.at[4, d], x_recv.at[4, d],
                device_id=(r, s, other_shard(d)), device_id_type=MESH,
            )

        for d in (2, 1, 3):
            along_copy(d).start()
        total = bwd_term[x].astype(f32)
        for d in (1, 3, 2):
            scatter_copy(bwd_term, bwd_got, 3, d).wait_recv()
            total = total + bwd_got[lax.rem(x + SHARDS - d, SHARDS)].astype(f32)
        for d in (1, 3, 2):
            along_copy(d).wait_recv()
            row = row + along_got[lax.rem(x + SHARDS - d, SHARDS)][:1, :]
        along = jnp.sum(jnp.where(diagonal, row, 0.0), axis=1, keepdims=True) * (1.0 / WIDTH)
        exact = fwd_all[x].astype(f32) * inverse
        result = up_own[...] + inverse * (total - exact * along)
        bwd_send[...] = pack_rows(result.reshape(REPLICAS, GROUP, FEATURES))
        for t in range(REPLICAS - 1, -1, -1):
            route_copy(bwd_send, peer(t), bwd_recv, 1, t, s - 1).start()
        for d in (1, 3, 2):
            scatter_copy(bwd_term, bwd_got, 3, d).wait_send()
            along_copy(d).wait_send()

    @pl.when(s > 1)
    def _():
        outer_b()

    outer_a()

    @pl.when(s >= 2)
    def _():
        relay(vb_recv, 2, relay_b, LATE_B, s - 2)
        relay(va_recv, 3, relay_a, LATE_A, s - 2)


    def outer_step(w, m, grad, factor, table, q_recv, v_recv, new_w, new_m):
        def body(k):
            partner = partners[s, table, k, r]
            weight = w[k].astype(f32)
            moment = m[k].astype(f32)
            own = momentum_decay * moment + factor * grad[k]
            new_moment = 0.5 * (own + v_recv[partner].astype(f32))
            kept = 0.5 * (weight + mix_rate * moment + q_recv[partner].astype(f32))
            new_w[k] = (kept - step_size * new_moment).astype(bf16)
            new_m[k] = new_moment.astype(bf16)

        each(REPLICAS, body)

    bulk_wait_recv(qb_recv, 0)
    bulk_wait_recv(vb_recv, 2)
    outer_step(wb, mb, grad_b, inner_rate * scale_out, 1, qb_recv, vb_recv, new_wb, new_mb)
    bulk_wait_recv(qa_recv, 1)
    bulk_wait_recv(va_recv, 3)
    outer_step(wa, ma, grad_a, inner_rate * scale_in, 0, qa_recv, va_recv, new_wa, new_ma)

    for d in (1, 2, 3):
        gather_copy(fwd_all, 0, d).wait_send()
        scatter_copy(fwd_term, fwd_got, 1, d).wait_send()
        gather_copy(bwd_all, 2, d).wait_send()

    @pl.when(s < SECTIONS - 1)
    def _():
        route_wait_send(fwd_send, 0)

    @pl.when(s > 0)
    def _():
        route_wait_send(bwd_send, 1)

    @pl.when(s >= 2)
    def _():
        relay_wait_send(2, relay_b, LATE_B)
        relay_wait_send(3, relay_a, LATE_A)

    @pl.when(s < 2)
    def _():
        relay_wait_send(0, relay_b, EARLY_B)
        relay_wait_send(1, relay_a, EARLY_A)

    for which, src in enumerate((qb_send, qa_send, vb_send, va_send)):
        bulk_wait_send(src, which)


def per_device(inputs, targets, weight_a, weight_b, moment_a, moment_b, routes, partners):
    def vmem(*shape, dtype=bf16):
        return pltpu.VMEM(shape, dtype)

    shards = (SHARDS, ROWS, FEATURES)
    routed = (REPLICAS, 2 * GROUP, 128)
    bulk_a = (REPLICAS, PIECE_A, HIDDEN)
    bulk_b = (REPLICAS, PIECE_B, WIDTH)
    dma = pltpu.SemaphoreType.DMA
    shape_a = pltpu.VMEM(bulk_a, bf16)
    shape_b = pltpu.VMEM(bulk_b, bf16)
    far = pl.BlockSpec(memory_space=pltpu.HBM)
    smem = pl.BlockSpec(memory_space=pltpu.SMEM)
    new_wa, new_wb, new_ma, new_mb = pl.pallas_call(
        kernel,
        out_shape=(shape_a, shape_b, shape_a, shape_b),
        in_specs=[far] * 6 + [smem, smem],
        out_specs=(pl.BlockSpec(memory_space=pltpu.VMEM),) * 4,
        scratch_shapes=[
            vmem(ROWS, FEATURES), vmem(ROWS, FEATURES),
            vmem(*bulk_a), vmem(*bulk_b), vmem(*bulk_a), vmem(*bulk_b),
            vmem(*shards), vmem(*shards), vmem(*shards), vmem(REPLICAS, GROUP, FEATURES, dtype=f32),
            vmem(*routed), vmem(*routed),
            vmem(*shards), vmem(*shards), vmem(*shards), vmem(*routed), vmem(*routed),
            vmem(8, ROWS, dtype=f32), vmem(SHARDS, 8, ROWS, dtype=f32),
            vmem(ROWS, FEATURES, dtype=f32),
            vmem(ROWS, 128, dtype=f32), vmem(ROWS, HIDDEN, dtype=f32),
            vmem(HIDDEN, ROWS), vmem(WIDTH, ROWS), vmem(ROWS, HIDDEN),
            vmem(*bulk_a, dtype=f32), vmem(*bulk_b, dtype=f32),
            vmem(*bulk_a), vmem(*bulk_b), vmem(*bulk_a), vmem(*bulk_b),
            vmem(*bulk_a), vmem(*bulk_b), vmem(*bulk_a), vmem(*bulk_b),
            pltpu.SMEM((REPLICAS,), jnp.int32), pltpu.SMEM((REPLICAS,), jnp.int32),
            pltpu.SMEM((REPLICAS,), jnp.int32),
            dma((6,)), dma((5, SHARDS)), dma((5, SHARDS)), dma((2,)), dma((2,)),
            dma((4,)), dma((4,)),
            vmem(2, PIECE_B, WIDTH), vmem(2, PIECE_A, HIDDEN),
            dma((4,)), dma((4,)), pltpu.SemaphoreType.REGULAR,
        ],
        compiler_params=pltpu.CompilerParams(
            collective_id=0, has_side_effects=True, vmem_limit_bytes=56 * 2**20
        ),
    )(
        inputs[0, 0], targets[0, 0], weight_a.reshape(bulk_a), weight_b.reshape(bulk_b),
        moment_a.reshape(bulk_a), moment_b.reshape(bulk_b), routes[0], partners,
    )
    return (
        new_wa.reshape(weight_a.shape), new_wb.reshape(weight_b.shape),
        new_ma.reshape(moment_a.shape), new_mb.reshape(moment_b.shape),
    )


def solution(mesh):
    placed = (
        P("replica", None, None, "shard"),
        P("replica", None, None, "shard"),
        P("replica", "section", None, "shard"),
        P("replica", "section", "shard", None),
        P("replica", "section", None, "shard"),
        P("replica", "section", "shard", None),
        P(),
        P(),
    )
    return jax.shard_map(
        per_device,
        mesh=mesh,
        in_specs=placed,
        out_specs=(
            P("replica", "section", None, "shard"),
            P("replica", "section", "shard", None),
            P("replica", "section", None, "shard"),
            P("replica", "section", "shard", None),
        ),
        check_vma=False,
    )
```

```python
import functools
import math

import jax
import jax.numpy as jnp
from jax import lax
from jax.experimental import pallas as pl
from jax.experimental.pallas import tpu as pltpu
from jax.sharding import PartitionSpec as P

MESH = pl.DeviceIdType.MESH
f32 = jnp.float32
bf16 = jnp.bfloat16

epsilon = 1e-05
inner_rate = 0.5
momentum_decay = 0.9
outer_rate = 0.7

step_size = outer_rate * (1.0 + momentum_decay)
mix_rate = step_size * momentum_decay - outer_rate * momentum_decay * momentum_decay

REPLICAS = 16
SECTIONS = 4
SHARDS = 4
ROWS = 128
GROUP = ROWS // REPLICAS
WIDTH = 1024
FEATURES = WIDTH // SHARDS
HIDDEN = 768
PIECE_A = WIDTH // REPLICAS
PIECE_B = HIDDEN // REPLICAS
scale_in = 1.0 / math.sqrt(WIDTH)
scale_out = 1.0 / math.sqrt(HIDDEN * SHARDS)

EARLY_B = (15,)
EARLY_A = (15,)
LATE_B = (15, 14)
LATE_A = (15,)
FIRST_Q = 7

NN = (((1,), (0,)), ((), ()))
NT = (((1,), (1,)), ((), ()))


def dot(a, b, dims=NN):
    return lax.dot_general(a, b, dims, preferred_element_type=f32)


def pack_rows(wide):
    return jnp.concatenate([wide[:, :, :128], wide[:, :, 128:]], axis=1).astype(bf16)


def unpack_rows(packed):
    wide = packed.astype(f32)
    count = wide.shape[0]
    return jnp.concatenate(
        [
            wide[:, :GROUP, :].reshape(count * GROUP, 128),
            wide[:, GROUP:, :].reshape(count * GROUP, 128),
        ],
        axis=1,
    )


def kernel(
    inp_h, tgt_h, wa_h, wb_h, ma_h, mb_h, routes, partners,
    new_wa, new_wb, new_ma, new_mb,
    inp, tgt, wa, wb, ma, mb,
    fwd_all, fwd_term, fwd_got, fwd_out, fwd_send, fwd_recv,
    bwd_all, bwd_term, bwd_got, bwd_send, bwd_recv, along_send, along_got, up_own,
    inv_rms, slope, hidden_t, normed_t, grad_pre, grad_a, grad_b,
    qa_send, qb_send, qa_recv, qb_recv, va_send, vb_send, va_recv, vb_recv,
    order_f, order_a, order_b,
    load_sem, x_send, x_recv, z_send, z_recv, bulk_send, bulk_recv,
    relay_b, relay_a, relay_send, relay_recv, clear,
):
    r = lax.axis_index("replica")
    s = lax.axis_index("section")
    x = lax.axis_index("shard")
    y, z = r // 8, lax.rem(r, 8)
    across = (1 - y) * 8 + z
    first, last = s == 0, s == SECTIONS - 1

    def other_shard(d):
        return lax.rem(x + d, SHARDS)

    def peer(t):
        dy, h = lax.rem(t, 2), t // 2
        odd = lax.rem(h, 2)
        dz = odd * ((h + 1) // 2) + (1 - odd) * lax.rem(8 - h // 2, 8)
        return lax.rem(y + dy, 2) * 8 + lax.rem(z + dz, 8)

    def each(count, body, start=0):
        def step(i, carry):
            body(i)
            return carry

        lax.fori_loop(start, count, step, 0)

    loads = [
        pltpu.make_async_copy(src, dst, load_sem.at[i])
        for i, (src, dst) in enumerate(
            [(inp_h, inp), (wa_h, wa), (wb_h, wb), (ma_h, ma), (mb_h, mb), (tgt_h, tgt)]
        )
    ]
    for copy in loads:
        copy.start()

    barrier = pltpu.get_barrier_semaphore()

    def greet(device):
        pl.semaphore_signal(barrier, inc=1, device_id=device, device_id_type=MESH)

    for d in (1, 2, 3):
        greet((r, s, other_shard(d)))

    @pl.when(s < SECTIONS - 1)
    def _():
        each(REPLICAS, lambda t: greet((peer(REPLICAS - 1 - t), s + 1, x)))

    @pl.when(s > 0)
    def _():
        each(REPLICAS, lambda t: greet((peer(REPLICAS - 1 - t), s - 1, x)))

    each(REPLICAS - 1, lambda t: greet((peer(REPLICAS - 1 - t), s, x)))

    other = lax.rem(s + 2, SECTIONS)
    greet((across, other, x))
    greet((lax.rem(z + 4, 8), other, x))
    greet((8 + lax.rem(z + 4, 8), other, x))


    def invert(table, out):
        def body(p):
            found = 0
            for g in range(REPLICAS):
                apart = table(g) - p
                found = jnp.maximum(found, g * (1 - jnp.minimum(apart * apart, 1)))
            out[p] = found

        each(REPLICAS, body)

    link = jnp.minimum(s, SECTIONS - 2)


    def fill_q(w, m, order, send, recv):
        def body(p):
            k = order[p]
            value = (w[k].astype(f32) + mix_rate * m[k].astype(f32)).astype(bf16)
            send[p] = value

        each(REPLICAS, body)
        recv[r] = send[r]

    def make_v(m, grad, factor, order, send):
        def body(p):
            k = order[p]
            value = momentum_decay * m[k].astype(f32) + factor * grad[k]
            send[p] = value.astype(bf16)

        return body

    def prepare_q(needed):
        invert(lambda g: partners[s, 0, g, r], order_a)
        invert(lambda g: partners[s, 1, g, r], order_b)
        for i in needed:
            loads[i].wait()
        fill_q(wb, mb, order_b, qb_send, qb_recv)
        fill_q(wa, ma, order_a, qa_send, qa_recv)

    @pl.when(s > 0)
    def _():
        prepare_q((2, 4, 1, 3))

    links = jnp.minimum(s, 1) + jnp.minimum(SECTIONS - 1 - s, 1)
    pl.semaphore_wait(barrier, SHARDS - 1 + REPLICAS - 1 + REPLICAS * links + 3)


    def gather_copy(ref, phase, d):
        return pltpu.make_async_remote_copy(
            ref.at[x], ref.at[x], x_send.at[phase, d], x_recv.at[phase, d],
            device_id=(r, s, other_shard(d)), device_id_type=MESH,
        )

    def scatter_copy(src, dst, phase, d):
        return pltpu.make_async_remote_copy(
            src.at[other_shard(d)], dst.at[x], x_send.at[phase, d], x_recv.at[phase, d],
            device_id=(r, s, other_shard(d)), device_id_type=MESH,
        )

    def route_copy(src, slot, dst, phase, t, section):
        return pltpu.make_async_remote_copy(
            src.at[slot], dst.at[r], z_send.at[phase], z_recv.at[phase],
            device_id=(peer(t), section, x), device_id_type=MESH,
        )

    def route_wait_recv(dst, phase):
        pltpu.make_async_copy(dst, dst, z_recv.at[phase]).wait()

    def route_wait_send(src, phase):
        pltpu.make_async_copy(src, src, z_send.at[phase]).wait()

    def bulk_start(src, dst, which, count=REPLICAS, make=None, skip=0, stop=None):
        def body(t):
            p = peer(t)
            if make is not None:
                make(p)
            pltpu.make_async_remote_copy(
                src.at[p], dst.at[r], bulk_send.at[which], bulk_recv.at[which],
                device_id=(p, s, x), device_id_type=MESH,
            ).start()

        each(count - 1 if stop is None else stop, lambda i: body(count - 1 - i), skip)

    def detour_start(src, which, buffer, relayed, section, make=None):
        for i, t in enumerate(relayed):
            if make is not None:
                make(peer(t))
            pltpu.make_async_remote_copy(
                src.at[peer(t)], buffer.at[i], bulk_send.at[which], relay_recv.at[which],
                device_id=(across, section, x), device_id_type=MESH,
            ).start()

    def relay(dst, which, buffer, relayed, section):
        if not relayed:
            return
        part = buffer.at[0 : len(relayed)]
        pltpu.make_async_copy(part, part, relay_recv.at[which]).wait()
        for i, t in enumerate(relayed):
            pltpu.make_async_remote_copy(
                buffer.at[i], dst.at[across], relay_send.at[which], bulk_recv.at[which],
                device_id=(lax.rem(1 - y + t % 2, 2) * 8 + lax.rem(z + 4, 8), section, x),
                device_id_type=MESH,
            ).start()

    def relay_wait_send(which, buffer, relayed):
        if not relayed:
            return
        part = buffer.at[0 : len(relayed)]
        pltpu.make_async_copy(part, part, relay_send.at[which]).wait()

    def direct(relayed, upper):
        return REPLICAS - len(relayed) * (s // 2 if upper else 1 - s // 2)

    def bulk_wait_recv(dst, which):
        part = dst.at[0 : REPLICAS - 1]
        pltpu.make_async_copy(part, part, bulk_recv.at[which]).wait()

    def bulk_wait_send(src, which):
        part = src.at[0 : REPLICAS - 1]
        pltpu.make_async_copy(part, part, bulk_send.at[which]).wait()

    def rows_a(j):
        span = FEATURES // PIECE_A
        return wa[pl.ds(j * span, span)].reshape(FEATURES, HIDDEN)

    def columns_b(j):
        columns = pl.ds(pl.multiple_of(j * FEATURES, FEATURES), FEATURES)
        return wb[:, :, columns].reshape(HIDDEN, FEATURES)


    loads[0].wait()

    @pl.when(first)
    def _():
        fwd_all[x] = inp[...]

    @pl.when(s > 0)
    def _():
        loads[5].wait()

    @pl.when(s >= 2)
    def _():
        detour_start(qb_send, 0, relay_b, EARLY_B, s - 2)
        detour_start(qa_send, 1, relay_a, EARLY_A, s - 2)
        bulk_start(qb_send, qb_recv, 0, direct(EARLY_B, True))

    @pl.when(last)
    def _():
        bulk_start(qa_send, qa_recv, 1, direct(EARLY_A, True))

    def relay_q():
        relay(qb_recv, 0, relay_b, EARLY_B, s + 2)
        relay(qa_recv, 1, relay_a, EARLY_A, s + 2)

    @pl.when(s > 0)
    def _():
        invert(lambda g: routes[link, r, g], order_f)
        route_wait_recv(fwd_recv, 0)
        fwd_all[x] = unpack_rows(fwd_recv[...]).astype(bf16)

    for d in (2, 1, 3):
        gather_copy(fwd_all, 0, d).start()

    @pl.when(first)
    def _():
        invert(lambda g: routes[link, r, g], order_f)
        loads[1].wait()
        loads[2].wait()
        loads[5].wait()

    preact = jnp.zeros((ROWS, HIDDEN), f32)
    square = jnp.zeros((ROWS, 1), f32)
    for d in (0, 1, 3, 2):
        if d:
            gather_copy(fwd_all, 0, d).wait_recv()
        j = lax.rem(x + SHARDS - d, SHARDS)
        part = fwd_all[j]
        preact = preact + dot(part, rows_a(j))
        wide = part.astype(f32)
        square = square + jnp.sum(wide * wide, axis=1, keepdims=True)
    inverse = lax.rsqrt(square * (1.0 / WIDTH) + epsilon)
    inv_rms[...] = jnp.broadcast_to(inverse, inv_rms.shape)
    preact = preact * (inverse * scale_in)
    gate = 1.0 / (1.0 + jnp.exp(-preact))
    hidden = (preact * gate).astype(bf16)
    for d in (2, 1, 3, 0):
        j = other_shard(d)
        fwd_term[j] = (dot(hidden, columns_b(j)) * scale_out).astype(bf16)
        if d:
            scatter_copy(fwd_term, fwd_got, 1, d).start()
    slope[...] = (gate * (1.0 + preact * (1.0 - gate))) * scale_out
    total = fwd_term[x].astype(f32)
    for d in (1, 3, 2):
        scatter_copy(fwd_term, fwd_got, 1, d).wait_recv()
        total = total + fwd_got[lax.rem(x + SHARDS - d, SHARDS)].astype(f32)
    output = (fwd_all[x].astype(f32) + total).astype(bf16).astype(f32)

    @pl.when(s < SECTIONS - 1)
    def _():
        fwd_out[...] = output.reshape(REPLICAS, GROUP, FEATURES)
        for t in range(REPLICAS - 1, -1, -1):
            block = fwd_out[order_f[peer(t)]]
            fwd_send[t] = pack_rows(block[None])[0]
            route_copy(fwd_send, t, fwd_recv, 0, t, s + 1).start()

    @pl.when(last)
    def _():
        up = (output - tgt[...].astype(f32)).astype(bf16)
        bwd_all[x] = up
        up_own[...] = up.astype(f32)
        for d in (2, 1, 3):
            gather_copy(bwd_all, 2, d).start()


    @pl.when(first)
    def _():
        prepare_q((3, 4))
        bulk_start(qb_send, qb_recv, 0, stop=FIRST_Q)
        pl.semaphore_wait(clear, 1)
        bulk_start(qb_send, qb_recv, 0, skip=FIRST_Q)

    @pl.when(s == 1)
    def _():
        pl.semaphore_signal(clear, inc=1, device_id=(r, 0, x), device_id_type=MESH)
        bulk_start(qb_send, qb_recv, 0)

    @pl.when(s < SECTIONS - 1)
    def _():
        bulk_start(qa_send, qa_recv, 1, direct(EARLY_A, True))

    @pl.when(s < 2)
    def _():
        relay_q()

    hidden_t[...] = hidden.T
    for j in range(SHARDS):
        normed = (fwd_all[j].astype(f32) * inverse).astype(bf16)
        normed_t[j * FEATURES : (j + 1) * FEATURES, :] = normed.T


    @pl.when(s < SECTIONS - 1)
    def _():
        route_wait_recv(bwd_recv, 1)
        for g in range(REPLICAS):
            block = bwd_recv[routes[link, r, g]]
            up_own[g * GROUP : (g + 1) * GROUP, :] = unpack_rows(block[None])
        bwd_all[x] = up_own[...].astype(bf16)
        for d in (2, 1, 3):
            gather_copy(bwd_all, 2, d).start()

    grad_hidden = jnp.zeros((ROWS, HIDDEN), f32)
    for d in (0, 1, 3, 2):
        if d:
            gather_copy(bwd_all, 2, d).wait_recv()
        j = lax.rem(x + SHARDS - d, SHARDS)
        grad_hidden = grad_hidden + dot(bwd_all[j], columns_b(j), NT)
    grad_pre[...] = (grad_hidden * slope[...]).astype(bf16)

    def outer_b():
        for j in range(SHARDS):
            value = dot(hidden_t[...], bwd_all[j]).reshape(REPLICAS, PIECE_B, FEATURES)
            grad_b[:, :, j * FEATURES : (j + 1) * FEATURES] = value
        make = make_v(mb, grad_b, inner_rate * scale_out, order_b, vb_send)
        @pl.when(s < 2)
        def _():
            detour_start(vb_send, 2, relay_b, LATE_B, s + 2, make)

        bulk_start(vb_send, vb_recv, 2, direct(LATE_B, False), make)
        make(r)
        vb_recv[r] = vb_send[r]

    def outer_a():
        for j in range(SHARDS):
            value = dot(normed_t[j * FEATURES : (j + 1) * FEATURES, :], grad_pre[...])
            span = FEATURES // PIECE_A
            grad_a[j * span : (j + 1) * span] = value.reshape(span, PIECE_A, HIDDEN)
        make = make_v(ma, grad_a, inner_rate * scale_in, order_a, va_send)

        @pl.when(s < 2)
        def _():
            detour_start(va_send, 3, relay_a, LATE_A, s + 2, make)

        bulk_start(va_send, va_recv, 3, direct(LATE_A, False), make)
        make(r)
        va_recv[r] = va_send[r]

    @pl.when(s <= 1)
    def _():
        outer_b()

    @pl.when(s > 0)
    def _():
        inverse = inv_rms[:, :1]
        share = jnp.zeros((ROWS, 1), f32)
        for d in (2, 1, 3, 0):
            j = other_shard(d)
            term = (dot(grad_pre[...], rows_a(j), NT) * scale_in).astype(bf16)
            bwd_term[j] = term
            if d:
                scatter_copy(bwd_term, bwd_got, 3, d).start()
            exact = fwd_all[j].astype(f32) * inverse
            share = share + jnp.sum(term.astype(f32) * exact, axis=1, keepdims=True)
        diagonal = lax.broadcasted_iota(jnp.int32, (ROWS, ROWS), 0) == lax.broadcasted_iota(
            jnp.int32, (ROWS, ROWS), 1
        )
        row = jnp.sum(jnp.where(diagonal, share, 0.0), axis=0, keepdims=True)
        along_send[...] = jnp.broadcast_to(row, along_send.shape)

        def along_copy(d):
            return pltpu.make_async_remote_copy(
                along_send, along_got.at[x], x_send.at[4, d], x_recv.at[4, d],
                device_id=(r, s, other_shard(d)), device_id_type=MESH,
            )

        for d in (2, 1, 3):
            along_copy(d).start()
        total = bwd_term[x].astype(f32)
        for d in (1, 3, 2):
            scatter_copy(bwd_term, bwd_got, 3, d).wait_recv()
            total = total + bwd_got[lax.rem(x + SHARDS - d, SHARDS)].astype(f32)
        for d in (1, 3, 2):
            along_copy(d).wait_recv()
            row = row + along_got[lax.rem(x + SHARDS - d, SHARDS)][:1, :]
        along = jnp.sum(jnp.where(diagonal, row, 0.0), axis=1, keepdims=True) * (1.0 / WIDTH)
        exact = fwd_all[x].astype(f32) * inverse
        result = up_own[...] + inverse * (total - exact * along)
        bwd_send[...] = pack_rows(result.reshape(REPLICAS, GROUP, FEATURES))
        for t in range(REPLICAS - 1, -1, -1):
            route_copy(bwd_send, peer(t), bwd_recv, 1, t, s - 1).start()
        for d in (1, 3, 2):
            scatter_copy(bwd_term, bwd_got, 3, d).wait_send()
            along_copy(d).wait_send()

    @pl.when(s > 1)
    def _():
        outer_b()

    outer_a()

    @pl.when(s >= 2)
    def _():
        relay(vb_recv, 2, relay_b, LATE_B, s - 2)
        relay(va_recv, 3, relay_a, LATE_A, s - 2)


    def outer_step(w, m, grad, factor, table, q_recv, v_recv, new_w, new_m):
        def body(k):
            partner = partners[s, table, k, r]
            weight = w[k].astype(f32)
            moment = m[k].astype(f32)
            own = momentum_decay * moment + factor * grad[k]
            new_moment = 0.5 * (own + v_recv[partner].astype(f32))
            kept = 0.5 * (weight + mix_rate * moment + q_recv[partner].astype(f32))
            new_w[k] = (kept - step_size * new_moment).astype(bf16)
            new_m[k] = new_moment.astype(bf16)

        each(REPLICAS, body)

    bulk_wait_recv(qb_recv, 0)
    bulk_wait_recv(vb_recv, 2)
    outer_step(wb, mb, grad_b, inner_rate * scale_out, 1, qb_recv, vb_recv, new_wb, new_mb)
    bulk_wait_recv(qa_recv, 1)
    bulk_wait_recv(va_recv, 3)
    outer_step(wa, ma, grad_a, inner_rate * scale_in, 0, qa_recv, va_recv, new_wa, new_ma)

    for d in (1, 2, 3):
        gather_copy(fwd_all, 0, d).wait_send()
        scatter_copy(fwd_term, fwd_got, 1, d).wait_send()
        gather_copy(bwd_all, 2, d).wait_send()

    @pl.when(s < SECTIONS - 1)
    def _():
        route_wait_send(fwd_send, 0)

    @pl.when(s > 0)
    def _():
        route_wait_send(bwd_send, 1)

    @pl.when(s >= 2)
    def _():
        relay_wait_send(2, relay_b, LATE_B)
        relay_wait_send(3, relay_a, LATE_A)

    @pl.when(s < 2)
    def _():
        relay_wait_send(0, relay_b, EARLY_B)
        relay_wait_send(1, relay_a, EARLY_A)

    for which, src in enumerate((qb_send, qa_send, vb_send, va_send)):
        bulk_wait_send(src, which)


def per_device(inputs, targets, weight_a, weight_b, moment_a, moment_b, routes, partners):
    def vmem(*shape, dtype=bf16):
        return pltpu.VMEM(shape, dtype)

    shards = (SHARDS, ROWS, FEATURES)
    routed = (REPLICAS, 2 * GROUP, 128)
    bulk_a = (REPLICAS, PIECE_A, HIDDEN)
    bulk_b = (REPLICAS, PIECE_B, WIDTH)
    dma = pltpu.SemaphoreType.DMA
    shape_a = pltpu.VMEM(bulk_a, bf16)
    shape_b = pltpu.VMEM(bulk_b, bf16)
    far = pl.BlockSpec(memory_space=pltpu.HBM)
    smem = pl.BlockSpec(memory_space=pltpu.SMEM)
    new_wa, new_wb, new_ma, new_mb = pl.pallas_call(
        kernel,
        out_shape=(shape_a, shape_b, shape_a, shape_b),
        in_specs=[far] * 6 + [smem, smem],
        out_specs=(pl.BlockSpec(memory_space=pltpu.VMEM),) * 4,
        scratch_shapes=[
            vmem(ROWS, FEATURES), vmem(ROWS, FEATURES),
            vmem(*bulk_a), vmem(*bulk_b), vmem(*bulk_a), vmem(*bulk_b),
            vmem(*shards), vmem(*shards), vmem(*shards), vmem(REPLICAS, GROUP, FEATURES, dtype=f32),
            vmem(*routed), vmem(*routed),
            vmem(*shards), vmem(*shards), vmem(*shards), vmem(*routed), vmem(*routed),
            vmem(8, ROWS, dtype=f32), vmem(SHARDS, 8, ROWS, dtype=f32),
            vmem(ROWS, FEATURES, dtype=f32),
            vmem(ROWS, 128, dtype=f32), vmem(ROWS, HIDDEN, dtype=f32),
            vmem(HIDDEN, ROWS), vmem(WIDTH, ROWS), vmem(ROWS, HIDDEN),
            vmem(*bulk_a, dtype=f32), vmem(*bulk_b, dtype=f32),
            vmem(*bulk_a), vmem(*bulk_b), vmem(*bulk_a), vmem(*bulk_b),
            vmem(*bulk_a), vmem(*bulk_b), vmem(*bulk_a), vmem(*bulk_b),
            pltpu.SMEM((REPLICAS,), jnp.int32), pltpu.SMEM((REPLICAS,), jnp.int32),
            pltpu.SMEM((REPLICAS,), jnp.int32),
            dma((6,)), dma((5, SHARDS)), dma((5, SHARDS)), dma((2,)), dma((2,)),
            dma((4,)), dma((4,)),
            vmem(2, PIECE_B, WIDTH), vmem(2, PIECE_A, HIDDEN),
            dma((4,)), dma((4,)), pltpu.SemaphoreType.REGULAR,
        ],
        compiler_params=pltpu.CompilerParams(
            collective_id=0, has_side_effects=True, vmem_limit_bytes=56 * 2**20
        ),
    )(
        inputs[0, 0], targets[0, 0], weight_a.reshape(bulk_a), weight_b.reshape(bulk_b),
        moment_a.reshape(bulk_a), moment_b.reshape(bulk_b), routes[0], partners,
    )
    return (
        new_wa.reshape(weight_a.shape), new_wb.reshape(weight_b.shape),
        new_ma.reshape(moment_a.shape), new_mb.reshape(moment_b.shape),
    )


def solution(mesh):
    placed = (
        P("replica", None, None, "shard"),
        P("replica", None, None, "shard"),
        P("replica", "section", None, "shard"),
        P("replica", "section", "shard", None),
        P("replica", "section", None, "shard"),
        P("replica", "section", "shard", None),
        P(),
        P(),
    )
    return jax.shard_map(
        per_device,
        mesh=mesh,
        in_specs=placed,
        out_specs=(
            P("replica", "section", None, "shard"),
            P("replica", "section", "shard", None),
            P("replica", "section", None, "shard"),
            P("replica", "section", "shard", None),
        ),
        check_vma=False,
    )
```
